256 devices in a mesh: src: 16 (over y, z_lo), tgt: 16 (over z_hi, x, core).
Axes of the slice: x: 4, y: 4, z: 8 (z_hi: 2, z_lo: 4; z = z_hi * 4 + z_lo), core: 2. Of those that a mesh axis runs over, the one named last changes fastest.
Arguments:
- edge_state: bfloat16 [16, 16, 1024, 512], P('src', 'tgt'), may hold values from -6 to 6
- edge_source: int32 [16, 16, 1024], P('src', 'tgt'), may hold values from 0 to 1023
- edge_target: int32 [16, 16, 1024], P('src', 'tgt'), may hold values from 0 to 1023
- live_edges: int32 [16, 16], P('src', 'tgt'), may hold values from 64 to 1024, as said below
- inner_one: bfloat16 [512, 512], replicated, may hold values from -0.25 to 0.25
- outer_one: bfloat16 [512, 512], replicated, may hold values from -0.25 to 0.25
- inner_two: bfloat16 [512, 512], replicated, may hold values from -0.25 to 0.25
- outer_two: bfloat16 [512, 512], replicated, may hold values from -0.25 to 0.25
- gain_one: float32 [512], replicated, may hold values from 0.1 to 1.9
- gain_two: float32 [512], replicated, may hold values from 0.1 to 1.9
Outputs:
- final_state: bfloat16 [16, 16, 1024, 512], P('src', 'tgt')
The draws below stay inside these ranges and needn't reach their ends.
Inputs may be any that keep to these rules, and one draw needn't show every extreme that they name: `edge_source`: source atoms within a block. `edge_target`: target atoms within a block. `live_edges`: a multiple of 64; some block pair is full in every draw.
All inputs are finite; a program needn't handle non-finite values.
Results may differ from the reference program's by a relative error of at most 0.013.
Values sent between devices are 32-bit elements; how exact they have to be, the bound alone decides.
A program may use at most 64 MiB of HBM per device.

```python
import jax
import jax.numpy as jnp
from jax import lax

C = 512
E_DEV = 1024
SRC_ATOMS = 1024
TGT_ATOMS = 1024
ATOMS = 16384
N_SRC = 16
N_TGT = 16


def draw_live_edges(key, part):
    key_steps, key_full = jax.random.split(key)
    multiples = jax.random.randint(key_steps, (N_SRC * N_TGT,), 1, 17)
    counts = E_DEV // 16 * multiples
    fullest = jax.random.randint(key_full, (), 0, N_SRC * N_TGT)
    counts = counts.at[fullest].set(E_DEV)
    return counts.reshape(N_SRC, N_TGT).astype(jnp.int32)


def set_ends(entries, rng, low, largest):
    spot = [jax.random.randint(jax.random.fold_in(rng, axis), (), 0, length) for axis, length in enumerate(entries.shape)]
    longest = entries.shape.index(max(entries.shape))
    next_to = spot[:longest] + [(spot[longest] + 1) % entries.shape[longest]] + spot[longest + 1:]
    return entries.at[tuple(spot)].set(low).at[tuple(next_to)].set(largest)


def levels(own_key, shape, cuts, least, largest):
    loudness = 1.0
    for dim, shards_of in cuts:
        draws = jax.random.uniform(jax.random.fold_in(jax.random.fold_in(own_key, 6), dim), (shards_of,), jnp.float32, least / len(cuts), largest / len(cuts))
        loudness = loudness * jnp.repeat(jnp.exp(draws), shape[dim] // shards_of).reshape((-1,) + (1,) * (len(shape) - 1 - dim))
    return loudness


def noise(key, shape, width, most, shards=(), kind=jnp.bfloat16):
    array = width * jax.random.normal(key, shape, jnp.float32)
    if shards:
        array = array * levels(key, shape, shards, -0.22, 0.18)
    return jnp.clip(array, -most, most).astype(kind)


def setup_inputs(seed: int = 0) -> dict:
    keys = jax.random.split(jax.random.key(seed), 11)
    edge_state = noise(keys[0], (N_SRC, N_TGT, E_DEV, C), 1.0, 6.0, ((0, 16), (1, 16)))
    edge_source = set_ends(jax.random.randint(keys[1], (N_SRC, N_TGT, E_DEV), 0, SRC_ATOMS), jax.random.fold_in(keys[1], 1), 0, SRC_ATOMS - 1).astype(jnp.int32)
    edge_target = set_ends(jax.random.randint(keys[2], (N_SRC, N_TGT, E_DEV), 0, TGT_ATOMS), jax.random.fold_in(keys[2], 1), 0, TGT_ATOMS - 1).astype(jnp.int32)
    live_edges = draw_live_edges(jax.random.fold_in(keys[10], 71), 0)
    inner_one = noise(keys[4], (C, C), C ** -0.5, 0.25)
    outer_one = noise(keys[5], (C, C), C ** -0.5, 0.25)
    inner_two = noise(keys[6], (C, C), C ** -0.5, 0.25)
    outer_two = noise(keys[7], (C, C), C ** -0.5, 0.25)
    gain_one = jnp.clip(1.0 + 0.18 * jax.random.normal(keys[8], (C,), jnp.float32), 0.1, 1.9)
    gain_two = jnp.clip(1.0 + 0.18 * jax.random.normal(keys[9], (C,), jnp.float32), 0.1, 1.9)
    return {"edge_state": edge_state, "edge_source": edge_source, "edge_target": edge_target, "live_edges": live_edges, "inner_one": inner_one, "outer_one": outer_one, "inner_two": inner_two, "outer_two": outer_two, "gain_one": gain_one, "gain_two": gain_two}


def update_edges(message, inner, outer, gain):
    mean_square = lax.optimization_barrier(jnp.mean(message * message, axis=-1, keepdims=True))
    normed = message * lax.rsqrt(mean_square + 1e-05) * gain.astype(jnp.float32)
    normed_low = normed.astype(jnp.bfloat16)
    activated = jax.nn.relu(jnp.dot(normed_low, inner, preferred_element_type=jnp.float32)).astype(jnp.bfloat16)
    return normed + jnp.dot(activated, outer, preferred_element_type=jnp.float32)

def reference(edge_state, edge_source, edge_target, live_edges, inner_one, outer_one, inner_two, outer_two, gain_one, gain_two):
    src_blocks, tgt_blocks, edge_rows, channels = edge_state.shape
    total_atoms = ATOMS
    alive = jnp.arange(edge_rows)[None, None, :] < live_edges[:, :, None]
    source_atom = edge_source + (jnp.arange(src_blocks) * SRC_ATOMS)[:, None, None].astype(edge_source.dtype)
    target_atom = edge_target + (jnp.arange(tgt_blocks) * TGT_ATOMS)[None, :, None].astype(edge_target.dtype)

    def accumulate(running, inputs):
        values, atom_index, keep_rows = inputs
        contributions = jnp.where(keep_rows[..., None], values.astype(jnp.float32), jnp.float32(0.0))
        added = jax.ops.segment_sum(contributions.reshape(-1, channels), atom_index.reshape(-1), num_segments=total_atoms)
        return (running + added, None)
    empty = jnp.zeros((total_atoms, channels), jnp.float32)
    incoming, _ = lax.scan(accumulate, empty, (edge_state, target_atom, alive))

    def layer_one(inputs):
        values, atom_index, keep_rows = inputs
        message = incoming[atom_index] - values.astype(jnp.float32)
        result = update_edges(message, inner_one, outer_one, gain_one)
        return jnp.where(keep_rows[..., None], result, jnp.float32(0.0)).astype(jnp.bfloat16)
    reverse_state = lax.map(layer_one, (edge_state, target_atom, alive))
    outgoing, _ = lax.scan(accumulate, empty, (reverse_state, source_atom, alive))

    def layer_two(inputs):
        values, atom_index, keep_rows = inputs
        message = outgoing[atom_index] - values.astype(jnp.float32)
        result = update_edges(message, inner_two, outer_two, gain_two)
        return jnp.where(keep_rows[..., None], result, jnp.float32(0.0)).astype(jnp.bfloat16)
    return lax.map(layer_two, (reverse_state, source_atom, alive))
```

```python
import functools

import jax
import jax.numpy as jnp
from jax import lax
from jax.experimental import pallas as pl
from jax.experimental.pallas import tpu as pltpu
from jax.sharding import PartitionSpec as P

MESH = pl.DeviceIdType.MESH
CHUNKS = 4
RING = 4
TILE = 256
BF16 = jnp.bfloat16
F32 = jnp.float32


class Copies:
    def __init__(self, send_sems, recv_sems):
        self.send_sems, self.recv_sems = send_sems, recv_sems
        self.made = []

    def start(self, src, dst, device):
        i = len(self.made)
        copy = pltpu.make_async_remote_copy(
            src_ref=src,
            dst_ref=dst,
            send_sem=self.send_sems.at[i],
            recv_sem=self.recv_sems.at[i],
            device_id=device,
            device_id_type=MESH,
        )
        copy.start()
        self.made.append(copy)
        return copy


def rows_at(offset, count):
    return pl.ds(pl.multiple_of(offset, count), count)


class Ring:
    def __init__(self, copies, me, after, before, base, half, relay, direct, second):
        self.copies, self.me, self.after, self.before = copies, me, after, before
        self.base, self.half = base, half
        self.relay, self.direct, self.second = relay, direct, second

    def at(self, step, part):
        shard = (self.me + step + RING) % RING
        return rows_at(self.base + shard * (2 * self.half) + part * self.half, self.half)

    def reduce_first(self, data):
        start = self.copies.start
        self.relays = [
            start(data.at[self.at(2, 0)], self.relay.at[0], self.after),
            start(data.at[self.at(2, 1)], self.relay.at[1], self.before),
        ]
        self.directs = [
            start(data.at[self.at(1, 1)], self.direct.at[0], self.after),
            start(data.at[self.at(-1, 0)], self.direct.at[1], self.before),
        ]

    def reduce_second(self, data):
        start = self.copies.start
        self.seconds = []
        for way, (step, device) in enumerate(((1, self.after), (-1, self.before))):
            self.relays[way].wait_recv()
            rows = self.at(step, way)
            data[rows] = data[rows] + self.relay[way]
            self.seconds.append(start(data.at[rows], self.second.at[way], device))

    def reduce_last(self, data):
        for copy in self.directs + self.seconds:
            copy.wait_recv()
        low = data[self.at(0, 0)] + self.second[0] + self.direct[1]
        high = data[self.at(0, 1)] + self.direct[0] + self.second[1]
        return low, high

    def gather_first(self, full):
        start = self.copies.start
        low, high = self.at(0, 0), self.at(0, 1)
        self.firsts = [
            start(full.at[low], full.at[low], self.after),
            start(full.at[high], full.at[high], self.before),
        ]
        self.others = [
            start(full.at[high], full.at[high], self.after),
            start(full.at[low], full.at[low], self.before),
        ]

    def gather_second(self, full):
        start = self.copies.start
        for way, (step, device) in enumerate(((-1, self.after), (1, self.before))):
            self.firsts[way].wait_recv()
            rows = self.at(step, way)
            self.others.append(start(full.at[rows], full.at[rows], device))

    def gather_last(self):
        for copy in self.others:
            copy.wait_recv()


def kernel(
    state_ref,
    source_ref,
    target_ref,
    live_ref,
    inner_one_ref,
    outer_one_ref,
    inner_two_ref,
    outer_two_ref,
    gain_one_ref,
    gain_two_ref,
    out_ref,
    part_one,
    part_two,
    full_one,
    full_two,
    message,
    reverse,
    high,
    low,
    column_one,
    column_two,
    relay_one,
    direct_one,
    second_one,
    shard_one,
    cross_one,
    relay_two,
    direct_two,
    second_two,
    pair_two,
    cross_two,
    send_sems,
    recv_sems,
):
    rows, channels = state_ref.shape
    atoms = part_one.shape[0]
    chunk = atoms // CHUNKS

    src, tgt = lax.axis_index("src"), lax.axis_index("tgt")
    y, z_lo = src // 4, src % 4
    z_hi, x, core = tgt // 8, (tgt // 2) % 4, tgt % 2
    y_after, y_before = (((y + 1) % 4) * 4 + z_lo, tgt), (((y + 3) % 4) * 4 + z_lo, tgt)
    parity = z_lo % 2
    z_near, z_far = (y * 4 + z_lo + 1 - 2 * parity, tgt), (y * 4 + (z_lo + 2) % 4, tgt)
    sibling = (src, tgt + 1 - 2 * core)
    x_after = (src, z_hi * 8 + ((x + 1) % 4) * 2 + core)
    x_before = (src, z_hi * 8 + ((x + 3) % 4) * 2 + core)
    z_across = (src, (1 - z_hi) * 8 + x * 2 + core)

    barrier = pltpu.get_barrier_semaphore()
    partners = (y_after, y_before, z_near, z_far, sibling, x_after, x_before, z_across)
    for device in partners:
        pl.semaphore_signal(barrier, inc=1, device_id=device, device_id_type=MESH)

    live = live_ref[0, 0]
    alive = lax.broadcasted_iota(jnp.int32, (1, rows), 1) < live
    target_row = jnp.where(alive, target_ref[...], -1)
    source_row = jnp.where(alive, source_ref[...], -1)

    def scatter(part, values_ref, index_row, k):
        atom = lax.broadcasted_iota(jnp.int32, (chunk, rows), 0) + k * chunk
        ones = jnp.where(atom == index_row, F32(1), F32(0)).astype(BF16)
        part[pl.ds(k * chunk, chunk)] = jnp.dot(ones, values_ref[...], preferred_element_type=F32)

    def gather(full, column, k):
        values = full[pl.ds(k * chunk, chunk)]
        upper = values.astype(BF16)
        high[...] = upper
        low[...] = (values - upper.astype(F32)).astype(BF16)

        @pl.loop(0, rows // TILE)
        def _(t):
            tile = rows_at(t * TILE, TILE)
            index = column[tile]
            lane = lax.broadcasted_iota(jnp.int32, index.shape, 1) + k * chunk
            ones = jnp.concatenate(
                [
                    jnp.where(index == lane + 128 * j, F32(1), F32(0)).astype(BF16)
                    for j in range(chunk // 128)
                ],
                axis=1,
            )
            total = jnp.dot(ones, high[...], preferred_element_type=F32)
            total = total + jnp.dot(ones, low[...], preferred_element_type=F32)
            if k == 0:
                message[tile] = total
            else:
                message[tile] = message[tile] + total

    def layer(values_ref, column, inner_ref, outer_ref, gain_ref, result_ref):
        @pl.loop(0, rows // TILE)
        def _(t):
            tile = rows_at(t * TILE, TILE)
            m = message[tile] - values_ref[tile].astype(F32)
            mean_square = jnp.mean(m * m, axis=-1, keepdims=True)
            normed = m * lax.rsqrt(mean_square + 1e-5) * gain_ref[...]
            activated = jnp.dot(normed.astype(BF16), inner_ref[...], preferred_element_type=F32)
            activated = jnp.maximum(activated, F32(0)).astype(BF16)
            result = normed + jnp.dot(activated, outer_ref[...], preferred_element_type=F32)
            keep = column[tile][:, :1] >= 0
            result_ref[tile] = jnp.where(keep, result, F32(0)).astype(BF16)

    copies = Copies(send_sems, recv_sems)

    scatter(part_one, state_ref, target_row, 0)
    pl.semaphore_wait(barrier, len(partners))

    class LayerOne:
        def __init__(self, k):
            self.k = k
            half = chunk // RING // 2
            self.half = half
            self.ring = Ring(
                copies, y, y_after, y_before, k * chunk, half, relay_one.at[k], direct_one.at[k], second_one.at[k]
            )
            self.steps = [self.s0, self.s1, self.s2, self.s3, self.s4, self.s5, self.s6, self.s7]

        def s0(self):
            if self.k > 0:
                scatter(part_one, state_ref, target_row, self.k)
            self.ring.reduce_first(part_one)

        def s1(self):
            self.ring.reduce_second(part_one)

        def s2(self):
            low_half, high_half = self.ring.reduce_last(part_one)
            k, half = self.k, self.half
            shard_one[k, 0:half] = low_half
            shard_one[k, half : 2 * half] = high_half
            self.near = copies.start(
                shard_one.at[k, rows_at((1 - parity) * half, half)], cross_one.at[k, 0], z_near
            )

        def s3(self):
            k, half = self.k, self.half
            self.near.wait_recv()
            mine = rows_at(parity * half, half)
            shard_one[k, mine] = shard_one[k, mine] + cross_one[k, 0]
            self.far = copies.start(shard_one.at[k, mine], cross_one.at[k, 1], z_far)

        def s4(self):
            k, half = self.k, self.half
            self.far.wait_recv()
            mine = rows_at(k * chunk + y * (2 * half) + parity * half, half)
            full_one[mine] = shard_one[k, rows_at(parity * half, half)] + cross_one[k, 1]
            self.back = copies.start(full_one.at[mine], full_one.at[mine], z_near)

        def s5(self):
            self.back.wait_recv()
            self.ring.gather_first(full_one)

        def s6(self):
            self.ring.gather_second(full_one)

        def s7(self):
            self.ring.gather_last()
            gather(full_one, column_one, self.k)

    class LayerTwo:
        def __init__(self, k):
            self.k = k
            side = chunk // 2
            self.side = side
            self.base = k * chunk + core * side
            half = side // RING // 2
            self.half = half
            self.ring = Ring(
                copies, x, x_after, x_before, self.base, half, relay_two.at[k], direct_two.at[k], second_two.at[k]
            )
            self.steps = [self.s0, self.s1, self.s2, self.s3, self.s4, self.s5, self.s6, self.s7]

        def s0(self):
            k = self.k
            scatter(part_two, reverse, source_row, k)
            theirs = rows_at(k * chunk + (1 - core) * self.side, self.side)
            self.pair = copies.start(part_two.at[theirs], pair_two.at[k], sibling)

        def s1(self):
            self.pair.wait_recv()
            mine = rows_at(self.base, self.side)
            part_two[mine] = part_two[mine] + pair_two[self.k]
            self.ring.reduce_first(part_two)

        def s2(self):
            self.ring.reduce_second(part_two)

        def s3(self):
            low_half, high_half = self.ring.reduce_last(part_two)
            low_rows, high_rows = self.ring.at(0, 0), self.ring.at(0, 1)
            part_two[low_rows] = low_half
            part_two[high_rows] = high_half
            self.own = rows_at(self.base + x * (2 * self.half), 2 * self.half)
            self.across = copies.start(part_two.at[self.own], cross_two.at[self.k], z_across)

        def s4(self):
            self.across.wait_recv()
            full_two[self.own] = part_two[self.own] + cross_two[self.k]
            self.ring.gather_first(full_two)

        def s5(self):
            self.ring.gather_second(full_two)

        def s6(self):
            self.ring.gather_last()
            mine = rows_at(self.base, self.side)
            self.back = copies.start(full_two.at[mine], full_two.at[mine], sibling)

        def s7(self):
            self.back.wait_recv()
            gather(full_two, column_two, self.k)

    def run(parts):
        n = len(parts[0].steps)
        for t in range(n + CHUNKS - 1):
            for k in range(CHUNKS):
                if 0 <= t - k < n:
                    parts[k].steps[t - k]()
            if t == 0 and parts[0].__class__ is LayerOne:
                column_one[...] = jnp.transpose(jnp.broadcast_to(target_row, (128, rows)))
                column_two[...] = jnp.transpose(jnp.broadcast_to(source_row, (128, rows)))

    run([LayerOne(k) for k in range(CHUNKS)])
    layer(state_ref, column_one, inner_one_ref, outer_one_ref, gain_one_ref, reverse)
    run([LayerTwo(k) for k in range(CHUNKS)])
    layer(reverse, column_two, inner_two_ref, outer_two_ref, gain_two_ref, out_ref)

    for copy in copies.made:
        copy.wait_send()


COPIES_PER_CHUNK = 6 + 3 + 6 + 1 + 6 + 1 + 6 + 1


def body(
    edge_state,
    edge_source,
    edge_target,
    live_edges,
    inner_one,
    outer_one,
    inner_two,
    outer_two,
    gain_one,
    gain_two,
):
    rows, channels = edge_state.shape[2:]
    atoms = 1024
    chunk = atoms // CHUNKS
    half_one, half_two = chunk // RING // 2, chunk // 2 // RING // 2
    vmem = pl.BlockSpec(memory_space=pltpu.VMEM)
    smem = pl.BlockSpec(memory_space=pltpu.SMEM)

    def piece(*shape):
        return pltpu.VMEM((CHUNKS, *shape, channels), F32)

    result = pl.pallas_call(
        kernel,
        out_shape=jax.ShapeDtypeStruct((rows, channels), BF16),
        in_specs=[vmem, vmem, vmem, smem] + [vmem] * 6,
        out_specs=vmem,
        scratch_shapes=[
            pltpu.VMEM((atoms, channels), F32),
            pltpu.VMEM((atoms, channels), F32),
            pltpu.VMEM((atoms, channels), F32),
            pltpu.VMEM((atoms, channels), F32),
            pltpu.VMEM((rows, channels), F32),
            pltpu.VMEM((rows, channels), BF16),
            pltpu.VMEM((chunk, channels), BF16),
            pltpu.VMEM((chunk, channels), BF16),
            pltpu.VMEM((rows, 128), jnp.int32),
            pltpu.VMEM((rows, 128), jnp.int32),
            piece(2, half_one),
            piece(2, half_one),
            piece(2, half_one),
            piece(2 * half_one),
            piece(2, half_one),
            piece(2, half_two),
            piece(2, half_two),
            piece(2, half_two),
            piece(chunk // 2),
            piece(2 * half_two),
            pltpu.SemaphoreType.DMA((COPIES_PER_CHUNK * CHUNKS,)),
            pltpu.SemaphoreType.DMA((COPIES_PER_CHUNK * CHUNKS,)),
        ],
        compiler_params=pltpu.CompilerParams(
            collective_id=0, has_side_effects=True, vmem_limit_bytes=48 * 2**20
        ),
    )(
        edge_state.reshape(rows, channels),
        edge_source.reshape(1, rows),
        edge_target.reshape(1, rows),
        live_edges,
        inner_one,
        outer_one,
        inner_two,
        outer_two,
        gain_one.reshape(1, channels),
        gain_two.reshape(1, channels),
    )
    return result.reshape(1, 1, rows, channels)


def solution(mesh):
    placed = (
        P("src", "tgt", None, None),
        P("src", "tgt", None),
        P("src", "tgt", None),
        P("src", "tgt"),
        P(),
        P(),
        P(),
        P(),
        P(),
        P(),
    )
    return jax.shard_map(
        body, mesh=mesh, in_specs=placed, out_specs=P("src", "tgt", None, None), check_vma=False
    )
```

```python
import functools

import jax
import jax.numpy as jnp
from jax import lax
from jax.experimental import pallas as pl
from jax.experimental.pallas import tpu as pltpu
from jax.sharding import PartitionSpec as P

MESH = pl.DeviceIdType.MESH
RING = 4
TILE = 512
BLOCK = 256
LANES = 128
BF16 = jnp.bfloat16
F32 = jnp.float32

KINDS_ONE = ('AA', 'AB', 'AB', 'AA', 'BB', 'BA', 'AA', 'BB')
ORDER_ONE = (4, 0, 2, 5, 1, 0, 7, 3, 1, 2, 6, 0, 3, 4, 1, 5, 2, 6, 0, 3, 4, 1, 7, 5, 2, 6, 4, 3, 0, 5, 7, 1, 2, 6, 7, 1, 0, 4, 3, 2, 1, 5, 6, 0, 1, 4, 4, 7, 2, 3, 5, 2, 1, 7, 6, 4, 0, 7, 5, 3, 7, 6, 2, 4, 5, 3, 7, 6)
ORDER_TWO = (0, 6, 1, 2, 0, 3, 4, 1, 2, 5, 0, 3, 1, 2, 4, 0, 3, 5, 1, 6, 7, 4, 2, 7, 5, 3, 4, 6, 7, 5, 1, 0, 6, 2, 7, 3, 1, 4, 0, 2, 5, 6, 4, 7, 0, 1, 5, 3, 4, 6, 2, 1, 7, 0, 5, 3, 2, 4, 6, 7, 3, 5, 6, 7)
PLACE_ONE = (1, 0, 2, 5, 3, 4, 7, 6)
PLACE_TWO = (1, 0, 2, 4, 3, 5, 6, 7)


class Copies:
    def __init__(self, inbox, send_sem, recv_sems):
        self.inbox, self.send_sem, self.recv_sems = inbox, send_sem, recv_sems
        self.groups = self.used = self.sent = 0

    def group(self):
        self.groups += 1
        return self.groups - 1

    def room(self, count):
        room = pl.ds(self.used, count)
        self.used += count
        return room

    def start(self, src, dst, device, group):
        self.sent += src.shape[0]
        pltpu.make_async_remote_copy(
            src_ref=src,
            dst_ref=dst,
            send_sem=self.send_sem,
            recv_sem=self.recv_sems.at[group],
            device_id=device,
            device_id_type=MESH,
        ).start()

    def push(self, ref, rows, device, group):
        self.start(ref.at[rows], ref.at[rows], device, group)

    def hand(self, ref, rows, count, device, group):
        room = self.room(count)
        self.start(ref.at[rows], self.inbox.at[room], device, group)
        return room

    def wait(self, sem, count):
        rows = self.inbox.at[pl.ds(0, count)]
        pltpu.make_async_copy(rows, rows, sem).wait()

    def arrived(self, group, count):
        self.wait(self.recv_sems.at[group], count)

    def all_sent(self):
        self.wait(self.send_sem, self.sent)


def rows_at(offset, count):
    return pl.ds(pl.multiple_of(offset, 8), count)


class Ring:
    def __init__(self, copies, me, after, before, base, shard_stride, part_stride, count):
        self.copies, self.me, self.after, self.before = copies, me, after, before
        self.base, self.shard_stride, self.part_stride, self.count = base, shard_stride, part_stride, count

    def at(self, step, part):
        shard = (self.me + step + RING) % RING
        return rows_at(self.base + shard * self.shard_stride + part * self.part_stride, self.count)

    def reduce_first(self, data):
        self.relay_group, self.reduce_group = self.copies.group(), self.copies.group()

        def hand(step, part, device, group):
            return self.copies.hand(data, self.at(step, part), self.count, device, group)

        self.relays = [hand(2, 0, self.after, self.relay_group), hand(2, 1, self.before, self.relay_group)]
        self.directs = [hand(1, 1, self.after, self.reduce_group), hand(-1, 0, self.before, self.reduce_group)]

    def reduce_second(self, data):
        self.copies.arrived(self.relay_group, 2 * self.count)
        self.seconds = []
        for way, (step, device) in enumerate(((1, self.after), (-1, self.before))):
            rows = self.at(step, way)
            data[rows] = data[rows] + self.copies.inbox[self.relays[way]]
            self.seconds.append(self.copies.hand(data, rows, self.count, device, self.reduce_group))

    def reduce_last(self, data):
        self.copies.arrived(self.reduce_group, 4 * self.count)
        inbox = self.copies.inbox
        for way in range(2):
            rows = self.at(0, way)
            data[rows] = data[rows] + inbox[self.directs[1 - way]] + inbox[self.seconds[way]]

    def gather_first(self, full):
        low, high = self.at(0, 0), self.at(0, 1)
        self.first_group, self.near_group, self.last_group = [self.copies.group() for _ in range(3)]
        push = self.copies.push
        push(full, low, self.after, self.first_group)
        push(full, high, self.before, self.first_group)
        push(full, high, self.after, self.near_group)
        push(full, low, self.before, self.near_group)

    def gather_second(self, full):
        self.copies.arrived(self.first_group, 2 * self.count)
        self.copies.push(full, self.at(-1, 0), self.after, self.last_group)
        self.copies.push(full, self.at(1, 1), self.before, self.last_group)

    def gather_near(self):
        self.copies.arrived(self.near_group, 2 * self.count)

    def gather_last(self):
        self.copies.arrived(self.last_group, 2 * self.count)


def kernel(
    state_hbm,
    source_hbm,
    target_hbm,
    live_hbm,
    inner_one_hbm,
    outer_one_hbm,
    inner_two_hbm,
    outer_two_hbm,
    gain_one_hbm,
    gain_two_hbm,
    out_ref,
    state_ref,
    source_ref,
    target_ref,
    live_ref,
    inner_one_ref,
    outer_one_ref,
    inner_two_ref,
    outer_two_ref,
    gain_one_ref,
    gain_two_ref,
    part_one,
    part_two,
    full_one,
    full_two,
    message,
    reverse,
    high,
    low,
    ones_one,
    ones_two,
    inbox,
    local_sems,
    send_sems,
    recv_sems,
):
    rows, channels = state_ref.shape
    atoms = part_one.shape[0]

    src, tgt = lax.axis_index("src"), lax.axis_index("tgt")
    y, z_lo = src // 4, src % 4
    z_hi, x, core = tgt // 8, (tgt // 2) % 4, tgt % 2
    y_after, y_before = (((y + 1) % 4) * 4 + z_lo, tgt), (((y + 3) % 4) * 4 + z_lo, tgt)
    parity = z_lo % 2
    z_near, z_far = (y * 4 + z_lo + 1 - 2 * parity, tgt), (y * 4 + (z_lo + 2) % 4, tgt)
    sibling = (src, tgt + 1 - 2 * core)
    x_after = (src, z_hi * 8 + ((x + 1) % 4) * 2 + core)
    x_before = (src, z_hi * 8 + ((x + 3) % 4) * 2 + core)
    z_across = (src, (1 - z_hi) * 8 + x * 2 + core)

    barrier = pltpu.get_barrier_semaphore()
    partners = (y_after, y_before, z_near, z_far, sibling, x_after, x_before, z_across)
    for device in partners:
        pl.semaphore_signal(barrier, inc=1, device_id=device, device_id_type=MESH)

    loads = []
    for i, (far, near) in enumerate(
        (
            (live_hbm, live_ref),
            (target_hbm, target_ref),
            (state_hbm, state_ref),
            (source_hbm, source_ref),
            (inner_one_hbm, inner_one_ref),
            (outer_one_hbm, outer_one_ref),
            (gain_one_hbm, gain_one_ref),
            (inner_two_hbm, inner_two_ref),
            (outer_two_hbm, outer_two_ref),
            (gain_two_hbm, gain_two_ref),
        )
    ):
        load = pltpu.make_async_copy(far, near, local_sems.at[i])
        load.start()
        loads.append(load)
    for load in loads[:3]:
        load.wait()

    live = live_ref[0, 0]
    alive = lax.broadcasted_iota(jnp.int32, (1, rows), 1) < live

    def index_of(index_ref):
        return jnp.where(alive, index_ref[...], -1)

    def scatter(part, values_ref, index_ref, block):
        atom = lax.broadcasted_iota(jnp.int32, (BLOCK, rows), 0) + block * BLOCK
        ones = jnp.where(atom == index_of(index_ref), F32(1), F32(0)).astype(BF16)
        part[pl.ds(block * BLOCK, BLOCK)] = jnp.dot(ones, values_ref[...], preferred_element_type=F32)

    def mark(ones_ref, index_ref):
        for t in range(rows // LANES):
            row = jnp.where(
                lax.broadcasted_iota(jnp.int32, (1, LANES), 1) + t * LANES < live,
                index_ref[:, pl.ds(t * LANES, LANES)],
                -1,
            )
            column = jnp.transpose(jnp.broadcast_to(row, (LANES, LANES)))
            lane = lax.broadcasted_iota(jnp.int32, (LANES, LANES), 1)
            for j in range(atoms // LANES):
                ones_ref[pl.ds(t * LANES, LANES), pl.ds(j * LANES, LANES)] = jnp.where(
                    column == lane + j * LANES, F32(1), F32(0)
                ).astype(BF16)

    def gather(full, ones_ref, block, values_ref, first):
        values = full[pl.ds(block * BLOCK, BLOCK)]
        upper = values.astype(BF16)
        high[...] = upper
        low[...] = (values - upper.astype(F32)).astype(BF16)

        for t in range(rows // TILE):
            tile = pl.ds(t * TILE, TILE)
            ones = ones_ref[tile, pl.ds(block * BLOCK, BLOCK)]
            total = jnp.dot(ones, high[...], preferred_element_type=F32)
            total = total + jnp.dot(ones, low[...], preferred_element_type=F32)
            if first:
                message[tile] = total - values_ref[tile].astype(F32)
            else:
                message[tile] = message[tile] + total

    def layer(inner_ref, outer_ref, gain_ref, result_ref):
        for t in range(rows // TILE):
            tile = pl.ds(t * TILE, TILE)
            m = message[tile]
            mean_square = jnp.mean(m * m, axis=-1, keepdims=True)
            normed = m * lax.rsqrt(mean_square + 1e-5) * gain_ref[...]
            activated = jnp.dot(normed.astype(BF16), inner_ref[...], preferred_element_type=F32)
            activated = jnp.maximum(activated, F32(0)).astype(BF16)
            result = normed + jnp.dot(activated, outer_ref[...], preferred_element_type=F32)
            keep = lax.broadcasted_iota(jnp.int32, (TILE, channels), 0) + t * TILE < live
            result_ref[tile] = jnp.where(keep, result, F32(0)).astype(BF16)

    copies = Copies(inbox, send_sems.at[0], recv_sems)

    class LayerOne:
        def __init__(self, kind, base, size):
            self.size = size
            reduce_kind, gather_kind = kind
            eighth = size // 8
            if reduce_kind == "A":
                shard_stride, part_stride = 2 * eighth, eighth
                self.reduce_ring = self.ring(base, shard_stride, part_stride, eighth)
                self.mine = rows_at(base + y * shard_stride + parity * part_stride, eighth)
                self.theirs = rows_at(base + y * shard_stride + (1 - parity) * part_stride, eighth)
                steps = [self.ring_first, self.ring_second, self.ring_then_near, self.near_then_far]
            else:
                shard_stride, part_stride = eighth, 4 * eighth
                self.reduce_ring = self.ring(base + parity * part_stride, shard_stride, eighth // 2, eighth // 2)
                self.mine = rows_at(base + y * shard_stride + parity * part_stride, eighth)
                self.upper = rows_at(base + parity * part_stride, part_stride)
                self.lower = rows_at(base + (1 - parity) * part_stride, part_stride)
                steps = [self.near_first, self.near_then_ring, self.ring_second, self.ring_then_far]
            if gather_kind == "A":
                self.gather_ring = self.ring(base, shard_stride, part_stride, eighth)
                steps += [self.far_then_near, self.near_then_gather, self.gather_second, self.gather_end]
            else:
                self.gather_ring = self.ring(
                    base + parity * part_stride, shard_stride, eighth // 2, eighth // 2
                )
                steps += [self.far_then_gather, self.gather_second, self.near_backs, self.last_backs, self.backs_end]
            self.steps = steps

            def shard(step):
                return rows_at(base + ((y + step) % RING) * shard_stride + parity * part_stride, eighth)

            self.shard = shard

        def ring(self, *where):
            return Ring(copies, y, y_after, y_before, *where)

        def ring_first(self):
            self.reduce_ring.reduce_first(part_one)

        def ring_second(self):
            self.reduce_ring.reduce_second(part_one)

        def hand(self, rows, count, device):
            group = copies.group()
            return group, copies.hand(part_one, rows, count, device, group), count

        def add(self, rows, handed, result):
            group, room, count = handed
            copies.arrived(group, count)
            result[rows] = part_one[rows] + inbox[room]

        def ring_then_near(self):
            self.reduce_ring.reduce_last(part_one)
            self.near = self.hand(self.theirs, self.size // 8, z_near)

        def near_then_far(self):
            self.add(self.mine, self.near, part_one)
            self.far = self.hand(self.mine, self.size // 8, z_far)

        def near_first(self):
            self.near = self.hand(self.lower, self.size // 2, z_near)

        def near_then_ring(self):
            self.add(self.upper, self.near, part_one)
            self.reduce_ring.reduce_first(part_one)

        def ring_then_far(self):
            self.reduce_ring.reduce_last(part_one)
            self.far = self.hand(self.mine, self.size // 8, z_far)

        def far_then_near(self):
            self.add(self.mine, self.far, full_one)
            self.back = copies.group()
            copies.push(full_one, self.mine, z_near, self.back)

        def near_then_gather(self):
            copies.arrived(self.back, self.size // 8)
            self.gather_ring.gather_first(full_one)

        def gather_second(self):
            self.gather_ring.gather_second(full_one)

        def gather_end(self):
            self.gather_ring.gather_near()
            self.gather_ring.gather_last()

        def far_then_gather(self):
            self.add(self.mine, self.far, full_one)
            self.gather_ring.gather_first(full_one)
            self.back = copies.group()
            copies.push(full_one, self.mine, z_near, self.back)

        def near_backs(self):
            self.gather_ring.gather_near()
            for step in (1, 3):
                copies.push(full_one, self.shard(step), z_near, self.back)

        def last_backs(self):
            self.gather_ring.gather_last()
            copies.push(full_one, self.shard(2), z_near, self.back)

        def backs_end(self):
            copies.arrived(self.back, self.size // 2)

    class LayerTwo:
        def __init__(self, base, size):
            side = size // 2
            self.side, self.eighth = side, side // 8
            self.ours, self.theirs = rows_at(base + core * side, side), rows_at(base + (1 - core) * side, side)
            self.own = rows_at(base + core * side + x * (2 * self.eighth), 2 * self.eighth)
            self.ring = Ring(
                copies, x, x_after, x_before, base + core * side, 2 * self.eighth, self.eighth, self.eighth
            )
            self.steps = [
                self.pair_first,
                self.pair_then_ring,
                self.ring_second,
                self.ring_then_across,
                self.across_then_gather,
                self.gather_second,
                self.gather_then_pair,
                self.pair_end,
            ]

        def pair_first(self):
            self.pair = copies.group()
            self.pair_room = copies.hand(part_two, self.theirs, self.side, sibling, self.pair)

        def pair_then_ring(self):
            copies.arrived(self.pair, self.side)
            part_two[self.ours] = part_two[self.ours] + inbox[self.pair_room]
            self.ring.reduce_first(part_two)

        def ring_second(self):
            self.ring.reduce_second(part_two)

        def ring_then_across(self):
            self.ring.reduce_last(part_two)
            self.across = copies.group()
            self.across_room = copies.hand(part_two, self.own, 2 * self.eighth, z_across, self.across)

        def across_then_gather(self):
            copies.arrived(self.across, 2 * self.eighth)
            full_two[self.own] = part_two[self.own] + inbox[self.across_room]
            self.ring.gather_first(full_two)

        def gather_second(self):
            self.ring.gather_second(full_two)

        def gather_then_pair(self):
            self.ring.gather_near()
            self.ring.gather_last()
            self.back = copies.group()
            copies.push(full_two, self.ours, sibling, self.back)

        def pair_end(self):
            copies.arrived(self.back, self.side)

    def run(chunks, order, places, scatter_block, gather_block, aside=None):
        per_block = BLOCK // (atoms // len(chunks))
        done = [0] * len(chunks)
        scattered, ended, gathered = set(), {}, 0
        for i, k in enumerate(order):
            if i == len(chunks) and aside is not None:
                aside()
            block = places[k] // per_block
            if block not in scattered:
                scattered.add(block)
                scatter_block(block)
            chunks[k].steps[done[k]]()
            done[k] += 1
            if done[k] == len(chunks[k].steps):
                ended[block] = ended.get(block, 0) + 1
                if ended[block] == per_block:
                    gather_block(block, gathered == 0)
                    gathered += 1
        assert all(d == len(c.steps) for d, c in zip(done, chunks))

    def scatter_one(block):
        scatter(part_one, state_ref, target_ref, block)
        if block == PLACE_ONE[ORDER_ONE[0]] // (BLOCK * len(KINDS_ONE) // atoms):
            pl.semaphore_wait(barrier, len(partners))

    size_one = atoms // len(KINDS_ONE)
    chunks_one = [LayerOne(kind, place * size_one, size_one) for kind, place in zip(KINDS_ONE, PLACE_ONE)]
    size_two = atoms // len(PLACE_TWO)
    chunks_two = [LayerTwo(place * size_two, size_two) for place in PLACE_TWO]

    def mark_both():
        for load in loads[3:]:
            load.wait()
        mark(ones_one, target_ref)
        mark(ones_two, source_ref)

    def gather_one(block, first):
        gather(full_one, ones_one, block, state_ref, first)

    run(chunks_one, ORDER_ONE, PLACE_ONE, scatter_one, gather_one, mark_both)
    copies.all_sent()
    copies.send_sem, copies.sent = send_sems.at[1], 0
    layer(inner_one_ref, outer_one_ref, gain_one_ref, reverse)

    def gather_two(block, first):
        gather(full_two, ones_two, block, reverse, first)

    run(
        chunks_two,
        ORDER_TWO,
        PLACE_TWO,
        lambda block: scatter(part_two, reverse, source_ref, block),
        gather_two,
    )
    layer(inner_two_ref, outer_two_ref, gain_two_ref, out_ref)

    copies.all_sent()
    assert copies.groups == GROUPS


GROUPS = 8 * (len(KINDS_ONE) + len(PLACE_TWO))


def body(
    edge_state,
    edge_source,
    edge_target,
    live_edges,
    inner_one,
    outer_one,
    inner_two,
    outer_two,
    gain_one,
    gain_two,
):
    rows, channels = edge_state.shape[2:]
    atoms = 1024
    operands = (
        edge_state.reshape(rows, channels),
        edge_source.reshape(1, rows),
        edge_target.reshape(1, rows),
        live_edges,
        inner_one,
        outer_one,
        inner_two,
        outer_two,
        gain_one.reshape(1, channels),
        gain_two.reshape(1, channels),
    )

    def copy_of(i, operand):
        space = pltpu.SMEM if i == 3 else pltpu.VMEM
        return space(operand.shape, operand.dtype)

    result = pl.pallas_call(
        kernel,
        out_shape=jax.ShapeDtypeStruct((rows, channels), BF16),
        in_specs=[pl.BlockSpec(memory_space=pltpu.HBM)] * len(operands),
        out_specs=pl.BlockSpec(memory_space=pltpu.VMEM),
        scratch_shapes=[copy_of(i, operand) for i, operand in enumerate(operands)]
        + [
            pltpu.VMEM((atoms, channels), F32),
            pltpu.VMEM((atoms, channels), F32),
            pltpu.VMEM((atoms, channels), F32),
            pltpu.VMEM((atoms, channels), F32),
            pltpu.VMEM((rows, channels), F32),
            pltpu.VMEM((rows, channels), BF16),
            pltpu.VMEM((BLOCK, channels), BF16),
            pltpu.VMEM((BLOCK, channels), BF16),
            pltpu.VMEM((rows, atoms), BF16),
            pltpu.VMEM((rows, atoms), BF16),
            pltpu.VMEM((2 * atoms, channels), F32),
            pltpu.SemaphoreType.DMA((len(operands),)),
            pltpu.SemaphoreType.DMA((2,)),
            pltpu.SemaphoreType.DMA((GROUPS,)),
        ],
        compiler_params=pltpu.CompilerParams(
            collective_id=0, has_side_effects=True, vmem_limit_bytes=56 * 2**20
        ),
    )(*operands)
    return result.reshape(1, 1, rows, channels)


def solution(mesh):
    placed = (
        P("src", "tgt", None, None),
        P("src", "tgt", None),
        P("src", "tgt", None),
        P("src", "tgt"),
        P(),
        P(),
        P(),
        P(),
        P(),
        P(),
    )
    return jax.shard_map(
        body, mesh=mesh, in_specs=placed, out_specs=P("src", "tgt", None, None), check_vma=False
    )
```

```python
import functools

import jax
import jax.numpy as jnp
from jax import lax
from jax.experimental import pallas as pl
from jax.experimental.pallas import tpu as pltpu
from jax.sharding import PartitionSpec as P

MESH = pl.DeviceIdType.MESH
RING = 4
TILE = 512
CHUNK = 128
BLOCK = 256
LANES = 128
BF16 = jnp.bfloat16
F32 = jnp.float32

KINDS_ONE = ('BA', 'AA', 'AA', 'BB', 'AB', 'AA', 'BA', 'AB')
KINDS_TWO = ('aA', 'aa', 'aa', 'aA', 'aa', 'aa', 'aa', 'aa')
ORDER_ONE = (6, 5, 7, 0, 5, 4, 7, 6, 5, 2, 3, 4, 6, 7, 0, 2, 5, 1, 4, 6, 0, 3, 7, 1, 2, 4, 5, 0, 3, 1, 6, 2, 7, 3, 5, 4, 1, 6, 7, 0, 2, 7, 5, 4, 3, 6, 1, 0, 7, 4, 3, 2, 4, 5, 1, 3, 0, 3, 2, 6, 7, 1, 4, 0, 3, 2, 1)
ORDER_TWO = (3, 1, 0, 6, 3, 7, 6, 1, 2, 5, 0, 2, 3, 4, 6, 5, 4, 1, 0, 7, 2, 3, 5, 6, 4, 1, 7, 3, 0, 2, 5, 1, 0, 4, 1, 6, 7, 2, 5, 6, 3, 2, 5, 4, 3, 0, 7, 4, 0, 7)
PLACE_ONE = (4, 7, 6, 5, 3, 0, 1, 2)
PLACE_TWO = (6, 0, 2, 4, 5, 3, 1, 7)


class Copies:
    def __init__(self, inbox, send_sem, recv_sems):
        self.inbox, self.send_sem, self.recv_sems = inbox, send_sem, recv_sems
        self.groups = self.used = self.sent = 0

    def group(self):
        self.groups += 1
        return self.groups - 1

    def room(self, count):
        room = pl.ds(self.used, count)
        self.used += count
        return room

    def start(self, src, dst, device, group):
        self.sent += src.shape[0]
        pltpu.make_async_remote_copy(
            src_ref=src,
            dst_ref=dst,
            send_sem=self.send_sem,
            recv_sem=self.recv_sems.at[group],
            device_id=device,
            device_id_type=MESH,
        ).start()

    def push(self, ref, rows, device, group):
        self.start(ref.at[rows], ref.at[rows], device, group)

    def hand(self, ref, rows, count, device, group):
        room = self.room(count)
        self.start(ref.at[rows], self.inbox.at[room], device, group)
        return room

    def wait(self, sem, count):
        rows = self.inbox.at[pl.ds(0, count)]
        pltpu.make_async_copy(rows, rows, sem).wait()

    def arrived(self, group, count):
        self.wait(self.recv_sems.at[group], count)

    def all_sent(self):
        self.wait(self.send_sem, self.sent)


def rows_at(offset, count):
    return pl.ds(pl.multiple_of(offset, 8), count)


class Ring:
    def __init__(self, copies, me, after, before, across, base, shard_stride, part_stride, count):
        self.copies, self.me, self.after, self.before, self.across = copies, me, after, before, across
        self.base, self.shard_stride, self.part_stride, self.count = base, shard_stride, part_stride, count

    def at(self, step, part):
        shard = (self.me + step + RING) % RING
        return rows_at(self.base + shard * self.shard_stride + part * self.part_stride, self.count)

    def reduce_first(self, data):
        self.relay_group, self.reduce_group = self.copies.group(), self.copies.group()

        def hand(step, part, device, group):
            return self.copies.hand(data, self.at(step, part), self.count, device, group)

        self.relays = [hand(2, 0, self.after, self.relay_group), hand(2, 1, self.before, self.relay_group)]
        self.directs = [hand(1, 1, self.after, self.reduce_group), hand(-1, 0, self.before, self.reduce_group)]

    def reduce_second(self, data):
        self.copies.arrived(self.relay_group, 2 * self.count)
        self.seconds = []
        for way, (step, device) in enumerate(((1, self.after), (-1, self.before))):
            rows = self.at(step, way)
            data[rows] = data[rows] + self.copies.inbox[self.relays[way]]
            self.seconds.append(self.copies.hand(data, rows, self.count, device, self.reduce_group))

    def reduce_last(self, data):
        self.copies.arrived(self.reduce_group, 4 * self.count)
        inbox = self.copies.inbox
        for way in range(2):
            rows = self.at(0, way)
            data[rows] = data[rows] + inbox[self.directs[1 - way]] + inbox[self.seconds[way]]

    def gather_first(self, full, apart=False):
        low, high = self.at(0, 0), self.at(0, 1)
        self.first_group, self.near_group = self.copies.group(), self.copies.group()
        self.last_group = self.copies.group() if apart else self.near_group
        push = self.copies.push
        push(full, low, self.after, self.first_group)
        push(full, high, self.before, self.first_group)
        push(full, high, self.after, self.near_group)
        push(full, low, self.before, self.near_group)

    def gather_second(self, full):
        self.copies.arrived(self.first_group, 2 * self.count)
        self.copies.push(full, self.at(-1, 0), self.after, self.last_group)
        self.copies.push(full, self.at(1, 1), self.before, self.last_group)

    def gather_near(self):
        self.copies.arrived(self.near_group, 2 * self.count)

    def gather_last(self):
        self.copies.arrived(self.last_group, 2 * self.count)

    def gather_rest(self):
        self.copies.arrived(self.near_group, 4 * self.count)

    def shard(self, step):
        return rows_at(self.base + (self.me + step + RING) % RING * self.shard_stride, 2 * self.count)

    def reduce_at_once(self, data):
        self.reduce_group = self.copies.group()
        self.terms = [
            self.copies.hand(data, self.shard(step), 2 * self.count, device, self.reduce_group)
            for step, device in ((1, self.after), (-1, self.before), (2, self.across))
        ]

    def reduce_at_once_last(self, data):
        self.copies.arrived(self.reduce_group, 6 * self.count)
        rows, inbox = self.shard(0), self.copies.inbox
        data[rows] = data[rows] + inbox[self.terms[0]] + inbox[self.terms[1]] + inbox[self.terms[2]]

    def gather_at_once(self, full):
        self.near_group = self.copies.group()
        for device in (self.after, self.before, self.across):
            self.copies.push(full, self.shard(0), device, self.near_group)

    def gather_at_once_last(self):
        self.copies.arrived(self.near_group, 6 * self.count)


def kernel(
    state_hbm,
    source_hbm,
    target_hbm,
    live_hbm,
    inner_one_hbm,
    outer_one_hbm,
    inner_two_hbm,
    outer_two_hbm,
    gain_one_hbm,
    gain_two_hbm,
    out_ref,
    state_ref,
    source_ref,
    target_ref,
    live_ref,
    inner_one_ref,
    outer_one_ref,
    inner_two_ref,
    outer_two_ref,
    gain_one_ref,
    gain_two_ref,
    part_one,
    part_two,
    full_one,
    full_two,
    message,
    reverse,
    terms,
    ones_one,
    ones_two,
    inbox,
    local_sems,
    send_sems,
    recv_sems,
):
    rows, channels = state_ref.shape
    atoms = part_one.shape[0]

    src, tgt = lax.axis_index("src"), lax.axis_index("tgt")
    y, z_lo = src // 4, src % 4
    z_hi, x, core = tgt // 8, (tgt // 2) % 4, tgt % 2
    y_after, y_before = (((y + 1) % 4) * 4 + z_lo, tgt), (((y + 3) % 4) * 4 + z_lo, tgt)
    parity = z_lo % 2
    z_near, z_far = (y * 4 + z_lo + 1 - 2 * parity, tgt), (y * 4 + (z_lo + 2) % 4, tgt)
    sibling = (src, tgt + 1 - 2 * core)
    x_after = (src, z_hi * 8 + ((x + 1) % 4) * 2 + core)
    x_before = (src, z_hi * 8 + ((x + 3) % 4) * 2 + core)
    x_across = (src, z_hi * 8 + ((x + 2) % 4) * 2 + core)
    z_across = (src, (1 - z_hi) * 8 + x * 2 + core)

    barrier = pltpu.get_barrier_semaphore()
    partners = (y_after, y_before, z_near, z_far, sibling, x_after, x_before, x_across, z_across)
    for device in partners:
        pl.semaphore_signal(barrier, inc=1, device_id=device, device_id_type=MESH)

    loads = []
    for i, (far, near) in enumerate(
        (
            (live_hbm, live_ref),
            (target_hbm, target_ref),
            (state_hbm, state_ref),
            (source_hbm, source_ref),
            (inner_one_hbm, inner_one_ref),
            (outer_one_hbm, outer_one_ref),
            (gain_one_hbm, gain_one_ref),
            (inner_two_hbm, inner_two_ref),
            (outer_two_hbm, outer_two_ref),
            (gain_two_hbm, gain_two_ref),
        )
    ):
        load = pltpu.make_async_copy(far, near, local_sems.at[i])
        load.start()
        loads.append(load)
    for load in loads[:3]:
        load.wait()

    live = live_ref[0, 0]
    alive = lax.broadcasted_iota(jnp.int32, (1, rows), 1) < live

    def index_of(index_ref):
        return jnp.where(alive, index_ref[...], -1)

    def scatter(part, values_ref, index_ref, block):
        atom = lax.broadcasted_iota(jnp.int32, (BLOCK, rows), 0) + block * BLOCK
        ones = jnp.where(atom == index_of(index_ref), F32(1), F32(0)).astype(BF16)
        part[pl.ds(block * BLOCK, BLOCK)] = jnp.dot(ones, values_ref[...], preferred_element_type=F32)

    def mark(ones_ref, index_ref):
        for t in range(rows // LANES):
            row = jnp.where(
                lax.broadcasted_iota(jnp.int32, (1, LANES), 1) + t * LANES < live,
                index_ref[:, pl.ds(t * LANES, LANES)],
                -1,
            )
            column = jnp.transpose(jnp.broadcast_to(row, (LANES, LANES)))
            lane = lax.broadcasted_iota(jnp.int32, (LANES, LANES), 1)
            for j in range(atoms // LANES):
                ones_ref[pl.ds(t * LANES, LANES), pl.ds(j * LANES, LANES)] = jnp.where(
                    column == lane + j * LANES, F32(1), F32(0)
                ).astype(BF16)

    def pick(full, ones_ref, place, t):
        ones = ones_ref[pl.ds(t * TILE, TILE), pl.ds(place * CHUNK, CHUNK)]
        return jnp.dot(jnp.concatenate([ones, ones], axis=1), terms[...], preferred_element_type=F32)

    def split(full, place):
        values = full[pl.ds(place * CHUNK, CHUNK)]
        upper = values.astype(BF16)
        terms[pl.ds(0, CHUNK)] = upper
        terms[pl.ds(CHUNK, CHUNK)] = (values - upper.astype(F32)).astype(BF16)

    def gather(full, ones_ref, place, values_ref, first):
        split(full, place)
        for t in range(rows // TILE):
            tile = pl.ds(t * TILE, TILE)
            total = pick(full, ones_ref, place, t)
            if first:
                message[tile] = total - values_ref[tile].astype(F32)
            else:
                message[tile] = message[tile] + total

    def layer(full, ones_ref, place, inner_ref, outer_ref, gain_ref, result_ref):
        split(full, place)
        for t in range(rows // TILE):
            tile = pl.ds(t * TILE, TILE)
            m = message[tile] + pick(full, ones_ref, place, t)
            mean_square = jnp.mean(m * m, axis=-1, keepdims=True)
            normed = m * lax.rsqrt(mean_square + 1e-5) * gain_ref[...]
            activated = jnp.dot(normed.astype(BF16), inner_ref[...], preferred_element_type=F32)
            activated = jnp.maximum(activated, F32(0)).astype(BF16)
            result = normed + jnp.dot(activated, outer_ref[...], preferred_element_type=F32)
            keep = lax.broadcasted_iota(jnp.int32, (TILE, channels), 0) + t * TILE < live
            result_ref[tile] = jnp.where(keep, result, F32(0)).astype(BF16)

    copies = Copies(inbox, send_sems.at[0], recv_sems)

    class LayerOne:
        def __init__(self, kind, base, size):
            self.size = size
            reduce_kind, gather_kind = kind
            eighth = size // 8
            if reduce_kind == "A":
                shard_stride, part_stride = 2 * eighth, eighth
                self.reduce_ring = self.ring(base, shard_stride, part_stride, eighth)
                self.mine = rows_at(base + y * shard_stride + parity * part_stride, eighth)
                self.theirs = rows_at(base + y * shard_stride + (1 - parity) * part_stride, eighth)
                steps = [self.ring_first, self.ring_second, self.ring_then_near, self.near_then_far]
            else:
                shard_stride, part_stride = eighth, 4 * eighth
                self.reduce_ring = self.ring(base + parity * part_stride, shard_stride, eighth // 2, eighth // 2)
                self.mine = rows_at(base + y * shard_stride + parity * part_stride, eighth)
                self.upper = rows_at(base + parity * part_stride, part_stride)
                self.lower = rows_at(base + (1 - parity) * part_stride, part_stride)
                steps = [self.near_first, self.near_then_ring, self.ring_second, self.ring_then_far]
            if gather_kind == "A":
                self.gather_ring = self.ring(base, shard_stride, part_stride, eighth)
                steps += [self.far_then_near, self.near_then_gather, self.gather_second, self.gather_end]
            else:
                self.gather_ring = self.ring(
                    base + parity * part_stride, shard_stride, eighth // 2, eighth // 2
                )
                steps += [self.far_then_gather, self.gather_second, self.near_backs, self.last_backs, self.backs_end]
            self.steps = steps

            def shard(step):
                return rows_at(base + ((y + step) % RING) * shard_stride + parity * part_stride, eighth)

            self.shard = shard

        def ring(self, *where):
            return Ring(copies, y, y_after, y_before, None, *where)

        def ring_first(self):
            self.reduce_ring.reduce_first(part_one)

        def ring_second(self):
            self.reduce_ring.reduce_second(part_one)

        def hand(self, rows, count, device):
            group = copies.group()
            return group, copies.hand(part_one, rows, count, device, group), count

        def add(self, rows, handed, result):
            group, room, count = handed
            copies.arrived(group, count)
            result[rows] = part_one[rows] + inbox[room]

        def ring_then_near(self):
            self.reduce_ring.reduce_last(part_one)
            self.near = self.hand(self.theirs, self.size // 8, z_near)

        def near_then_far(self):
            self.add(self.mine, self.near, part_one)
            self.far = self.hand(self.mine, self.size // 8, z_far)

        def near_first(self):
            self.near = self.hand(self.lower, self.size // 2, z_near)

        def near_then_ring(self):
            self.add(self.upper, self.near, part_one)
            self.reduce_ring.reduce_first(part_one)

        def ring_then_far(self):
            self.reduce_ring.reduce_last(part_one)
            self.far = self.hand(self.mine, self.size // 8, z_far)

        def far_then_near(self):
            self.add(self.mine, self.far, full_one)
            self.back = copies.group()
            copies.push(full_one, self.mine, z_near, self.back)

        def near_then_gather(self):
            copies.arrived(self.back, self.size // 8)
            self.gather_ring.gather_first(full_one)

        def gather_second(self):
            self.gather_ring.gather_second(full_one)

        def gather_end(self):
            self.gather_ring.gather_rest()

        def far_then_gather(self):
            self.add(self.mine, self.far, full_one)
            self.gather_ring.gather_first(full_one, apart=True)
            self.back = copies.group()
            copies.push(full_one, self.mine, z_near, self.back)

        def near_backs(self):
            self.gather_ring.gather_near()
            for step in (1, 3):
                copies.push(full_one, self.shard(step), z_near, self.back)

        def last_backs(self):
            self.gather_ring.gather_last()
            copies.push(full_one, self.shard(2), z_near, self.back)

        def backs_end(self):
            copies.arrived(self.back, self.size // 2)

    class LayerTwo:
        def __init__(self, kind, base, size):
            side = size // 2
            self.side, self.eighth = side, side // 8
            self.ours, self.theirs = rows_at(base + core * side, side), rows_at(base + (1 - core) * side, side)
            self.own = rows_at(base + core * side + x * (2 * self.eighth), 2 * self.eighth)
            self.ring = Ring(
                copies, x, x_after, x_before, x_across, base + core * side, 2 * self.eighth, self.eighth, self.eighth
            )
            reduce_kind, gather_kind = kind
            self.steps = [self.pair_first, self.pair_then_ring]
            if reduce_kind == "A":
                self.reduce_first, self.reduce_last = self.ring.reduce_first, self.ring.reduce_last
                self.steps.append(self.ring_second)
            else:
                self.reduce_first, self.reduce_last = self.ring.reduce_at_once, self.ring.reduce_at_once_last
            self.steps += [self.ring_then_across, self.across_then_gather]
            if gather_kind == "A":
                self.gather_first, self.gather_rest = self.ring.gather_first, self.ring.gather_rest
                self.steps.append(self.gather_second)
            else:
                self.gather_first, self.gather_rest = self.ring.gather_at_once, self.ring.gather_at_once_last
            self.steps += [self.gather_then_pair, self.pair_end]

        def pair_first(self):
            self.pair = copies.group()
            self.pair_room = copies.hand(part_two, self.theirs, self.side, sibling, self.pair)

        def pair_then_ring(self):
            copies.arrived(self.pair, self.side)
            part_two[self.ours] = part_two[self.ours] + inbox[self.pair_room]
            self.reduce_first(part_two)

        def ring_second(self):
            self.ring.reduce_second(part_two)

        def ring_then_across(self):
            self.reduce_last(part_two)
            self.across = copies.group()
            self.across_room = copies.hand(part_two, self.own, 2 * self.eighth, z_across, self.across)

        def across_then_gather(self):
            copies.arrived(self.across, 2 * self.eighth)
            full_two[self.own] = part_two[self.own] + inbox[self.across_room]
            self.gather_first(full_two)

        def gather_second(self):
            self.ring.gather_second(full_two)

        def gather_then_pair(self):
            self.gather_rest()
            self.back = copies.group()
            copies.push(full_two, self.ours, sibling, self.back)

        def pair_end(self):
            copies.arrived(self.back, self.side)

    def run(chunks, order, places, scatter_block, gather_chunk, aside=None):
        done = [0] * len(chunks)
        scattered, ended = set(), 0
        for i, k in enumerate(order):
            if i == len(chunks) and aside is not None:
                aside()
            block = places[k] * CHUNK // BLOCK
            if block not in scattered:
                scattered.add(block)
                scatter_block(block)
            chunks[k].steps[done[k]]()
            done[k] += 1
            if done[k] == len(chunks[k].steps):
                ended += 1
                if ended == len(chunks):
                    last = places[k]
                else:
                    gather_chunk(places[k], ended == 1)
        assert all(d == len(c.steps) for d, c in zip(done, chunks))
        return last

    def scatter_one(block):
        scatter(part_one, state_ref, target_ref, block)
        if block == PLACE_ONE[ORDER_ONE[0]] * CHUNK // BLOCK:
            pl.semaphore_wait(barrier, len(partners))

    chunks_one = [LayerOne(kind, place * CHUNK, CHUNK) for kind, place in zip(KINDS_ONE, PLACE_ONE)]
    chunks_two = [LayerTwo(kind, place * CHUNK, CHUNK) for kind, place in zip(KINDS_TWO, PLACE_TWO)]

    def mark_both():
        for load in loads[3:]:
            load.wait()
        mark(ones_one, target_ref)
        mark(ones_two, source_ref)

    last = run(
        chunks_one,
        ORDER_ONE,
        PLACE_ONE,
        scatter_one,
        lambda place, first: gather(full_one, ones_one, place, state_ref, first),
        mark_both,
    )
    layer(full_one, ones_one, last, inner_one_ref, outer_one_ref, gain_one_ref, reverse)
    copies.all_sent()
    copies.send_sem, copies.sent = send_sems.at[1], 0

    last = run(
        chunks_two,
        ORDER_TWO,
        PLACE_TWO,
        lambda block: scatter(part_two, reverse, source_ref, block),
        lambda place, first: gather(full_two, ones_two, place, reverse, first),
    )
    layer(full_two, ones_two, last, inner_two_ref, outer_two_ref, gain_two_ref, out_ref)

    copies.all_sent()
    assert copies.groups == GROUPS


def groups_of(kind):
    return 4 + (3 if kind[1] == "A" else 4)


def groups_of_two(kind):
    return 3 + (2 if kind[0] == "A" else 1) + (2 if kind[1] == "A" else 1)


GROUPS = sum(map(groups_of, KINDS_ONE)) + sum(map(groups_of_two, KINDS_TWO))


def body(
    edge_state,
    edge_source,
    edge_target,
    live_edges,
    inner_one,
    outer_one,
    inner_two,
    outer_two,
    gain_one,
    gain_two,
):
    rows, channels = edge_state.shape[2:]
    atoms = 1024
    operands = (
        edge_state.reshape(rows, channels),
        edge_source.reshape(1, rows),
        edge_target.reshape(1, rows),
        live_edges,
        inner_one,
        outer_one,
        inner_two,
        outer_two,
        gain_one.reshape(1, channels),
        gain_two.reshape(1, channels),
    )

    def copy_of(i, operand):
        space = pltpu.SMEM if i == 3 else pltpu.VMEM
        return space(operand.shape, operand.dtype)

    result = pl.pallas_call(
        kernel,
        out_shape=jax.ShapeDtypeStruct((rows, channels), BF16),
        in_specs=[pl.BlockSpec(memory_space=pltpu.HBM)] * len(operands),
        out_specs=pl.BlockSpec(memory_space=pltpu.VMEM),
        scratch_shapes=[copy_of(i, operand) for i, operand in enumerate(operands)]
        + [
            pltpu.VMEM((atoms, channels), F32),
            pltpu.VMEM((atoms, channels), F32),
            pltpu.VMEM((atoms, channels), F32),
            pltpu.VMEM((atoms, channels), F32),
            pltpu.VMEM((rows, channels), F32),
            pltpu.VMEM((rows, channels), BF16),
            pltpu.VMEM((2 * CHUNK, channels), BF16),
            pltpu.VMEM((rows, atoms), BF16),
            pltpu.VMEM((rows, atoms), BF16),
            pltpu.VMEM((2 * atoms, channels), F32),
            pltpu.SemaphoreType.DMA((len(operands),)),
            pltpu.SemaphoreType.DMA((2,)),
            pltpu.SemaphoreType.DMA((GROUPS,)),
        ],
        compiler_params=pltpu.CompilerParams(
            collective_id=0, has_side_effects=True, vmem_limit_bytes=56 * 2**20
        ),
    )(*operands)
    return result.reshape(1, 1, rows, channels)


def solution(mesh):
    placed = (
        P("src", "tgt", None, None),
        P("src", "tgt", None),
        P("src", "tgt", None),
        P("src", "tgt"),
        P(),
        P(),
        P(),
        P(),
        P(),
        P(),
    )
    return jax.shard_map(
        body, mesh=mesh, in_specs=placed, out_specs=P("src", "tgt", None, None), check_vma=False
    )
```

```python
import functools

import jax
import jax.numpy as jnp
from jax import lax
from jax.experimental import pallas as pl
from jax.experimental.pallas import tpu as pltpu
from jax.sharding import PartitionSpec as P

MESH = pl.DeviceIdType.MESH
RING = 4
TILE = 512
CHUNK = 128
BLOCK = 256
LANES = 128
BF16 = jnp.bfloat16
F32 = jnp.float32

KINDS_ONE = ('BA', 'AA', 'AA', 'BB', 'AB', 'AA', 'BA', 'AB')
KINDS_TWO = ('aA', 'aa', 'aa', 'aA', 'aa', 'aa', 'aa', 'aa')
ORDER_ONE = (6, 5, 7, 0, 5, 4, 7, 6, 5, 2, 3, 4, 6, 7, 0, 2, 5, 1, 4, 6, 0, 3, 7, 1, 2, 4, 5, 0, 3, 1, 6, 2, 7, 3, 5, 4, 1, 6, 7, 0, 2, 7, 5, 4, 3, 6, 1, 0, 7, 4, 3, 2, 4, 5, 5, 1, 3, 0, 3, 2, 6, 6, 7, 7, 1, 4, 4, 0, 0, 3, 3, 2, 2, 1, 1)
ORDER_TWO = (3, 1, 0, 6, 3, 7, 6, 1, 2, 5, 0, 2, 3, 4, 6, 5, 4, 1, 0, 7, 2, 3, 5, 6, 4, 1, 7, 3, 0, 2, 5, 1, 0, 4, 1, 1, 6, 7, 2, 5, 6, 6, 3, 2, 2, 5, 5, 4, 3, 3, 0, 7, 4, 4, 0, 0, 7, 7)
PLACE_ONE = (3, 7, 5, 6, 4, 1, 0, 2)
PLACE_TWO = (2, 1, 5, 0, 7, 6, 3, 4)


class Copies:
    def __init__(self, inbox, send_sem, recv_sems):
        self.inbox, self.send_sem, self.recv_sems = inbox, send_sem, recv_sems
        self.groups = self.used = self.sent = 0

    def group(self):
        self.groups += 1
        return self.groups - 1

    def room(self, count):
        room = pl.ds(self.used, count)
        self.used += count
        return room

    def start(self, src, dst, device, group):
        self.sent += src.shape[0]
        pltpu.make_async_remote_copy(
            src_ref=src,
            dst_ref=dst,
            send_sem=self.send_sem,
            recv_sem=self.recv_sems.at[group],
            device_id=device,
            device_id_type=MESH,
        ).start()

    def push(self, ref, rows, device, group):
        self.start(ref.at[rows], ref.at[rows], device, group)

    def hand(self, ref, rows, count, device, group):
        room = self.room(count)
        self.start(ref.at[rows], self.inbox.at[room], device, group)
        return room

    def wait(self, sem, count):
        rows = self.inbox.at[pl.ds(0, count)]
        pltpu.make_async_copy(rows, rows, sem).wait()

    def arrived(self, group, count):
        self.wait(self.recv_sems.at[group], count)

    def all_sent(self):
        self.wait(self.send_sem, self.sent)


def rows_at(offset, count):
    return pl.ds(pl.multiple_of(offset, 8), count)


class Ring:
    def __init__(self, copies, me, after, before, across, base, shard_stride, part_stride, count):
        self.copies, self.me, self.after, self.before, self.across = copies, me, after, before, across
        self.base, self.shard_stride, self.part_stride, self.count = base, shard_stride, part_stride, count

    def at(self, step, part):
        shard = (self.me + step + RING) % RING
        return rows_at(self.base + shard * self.shard_stride + part * self.part_stride, self.count)

    def reduce_first(self, data):
        self.relay_group, self.reduce_group = self.copies.group(), self.copies.group()

        def hand(step, part, device, group):
            return self.copies.hand(data, self.at(step, part), self.count, device, group)

        self.relays = [hand(2, 0, self.after, self.relay_group), hand(2, 1, self.before, self.relay_group)]
        self.directs = [hand(1, 1, self.after, self.reduce_group), hand(-1, 0, self.before, self.reduce_group)]

    def reduce_second(self, data):
        self.copies.arrived(self.relay_group, 2 * self.count)
        self.seconds = []
        for way, (step, device) in enumerate(((1, self.after), (-1, self.before))):
            rows = self.at(step, way)
            data[rows] = data[rows] + self.copies.inbox[self.relays[way]]
            self.seconds.append(self.copies.hand(data, rows, self.count, device, self.reduce_group))

    def reduce_last(self, data):
        self.copies.arrived(self.reduce_group, 4 * self.count)
        inbox = self.copies.inbox
        for way in range(2):
            rows = self.at(0, way)
            data[rows] = data[rows] + inbox[self.directs[1 - way]] + inbox[self.seconds[way]]

    def gather_first(self, full, apart=False):
        low, high = self.at(0, 0), self.at(0, 1)
        self.first_group, self.near_group = self.copies.group(), self.copies.group()
        self.last_group = self.copies.group() if apart else self.near_group
        push = self.copies.push
        push(full, low, self.after, self.first_group)
        push(full, high, self.before, self.first_group)
        push(full, high, self.after, self.near_group)
        push(full, low, self.before, self.near_group)

    def gather_second(self, full):
        self.copies.arrived(self.first_group, 2 * self.count)
        self.copies.push(full, self.at(-1, 0), self.after, self.last_group)
        self.copies.push(full, self.at(1, 1), self.before, self.last_group)

    def gather_near(self):
        self.copies.arrived(self.near_group, 2 * self.count)

    def gather_last(self):
        self.copies.arrived(self.last_group, 2 * self.count)

    def gather_rest(self):
        self.copies.arrived(self.near_group, 4 * self.count)

    def shard(self, step):
        return rows_at(self.base + (self.me + step + RING) % RING * self.shard_stride, 2 * self.count)

    def reduce_at_once(self, data):
        self.reduce_group = self.copies.group()
        self.terms = [
            self.copies.hand(data, self.shard(step), 2 * self.count, device, self.reduce_group)
            for step, device in ((1, self.after), (-1, self.before), (2, self.across))
        ]

    def reduce_at_once_last(self, data):
        self.copies.arrived(self.reduce_group, 6 * self.count)
        rows, inbox = self.shard(0), self.copies.inbox
        data[rows] = data[rows] + inbox[self.terms[0]] + inbox[self.terms[1]] + inbox[self.terms[2]]

    def gather_at_once(self, full):
        self.near_group = self.copies.group()
        for device in (self.after, self.before, self.across):
            self.copies.push(full, self.shard(0), device, self.near_group)

    def gather_at_once_last(self):
        self.copies.arrived(self.near_group, 6 * self.count)


def kernel(
    state_hbm,
    source_hbm,
    target_hbm,
    live_hbm,
    inner_one_hbm,
    outer_one_hbm,
    inner_two_hbm,
    outer_two_hbm,
    gain_one_hbm,
    gain_two_hbm,
    out_hbm,
    state_ref,
    source_ref,
    target_ref,
    live_ref,
    inner_one_ref,
    outer_one_ref,
    inner_two_ref,
    outer_two_ref,
    gain_one_ref,
    gain_two_ref,
    part_one,
    part_two,
    full_one,
    full_two,
    message,
    reverse,
    final,
    terms,
    ones_one,
    ones_two,
    inbox,
    local_sems,
    send_sems,
    recv_sems,
):
    rows, channels = state_ref.shape
    atoms = part_one.shape[0]

    src, tgt = lax.axis_index("src"), lax.axis_index("tgt")
    y, z_lo = src // 4, src % 4
    z_hi, x, core = tgt // 8, (tgt // 2) % 4, tgt % 2
    y_after, y_before = (((y + 1) % 4) * 4 + z_lo, tgt), (((y + 3) % 4) * 4 + z_lo, tgt)
    parity = z_lo % 2
    z_near, z_far = (y * 4 + z_lo + 1 - 2 * parity, tgt), (y * 4 + (z_lo + 2) % 4, tgt)
    sibling = (src, tgt + 1 - 2 * core)
    x_after = (src, z_hi * 8 + ((x + 1) % 4) * 2 + core)
    x_before = (src, z_hi * 8 + ((x + 3) % 4) * 2 + core)
    x_across = (src, z_hi * 8 + ((x + 2) % 4) * 2 + core)
    z_across = (src, (1 - z_hi) * 8 + x * 2 + core)

    barrier = pltpu.get_barrier_semaphore()
    partners = (y_after, y_before, z_near, z_far, sibling, x_after, x_before, x_across, z_across)
    for device in partners:
        pl.semaphore_signal(barrier, inc=1, device_id=device, device_id_type=MESH)

    loads = []
    for i, (far, near) in enumerate(
        (
            (live_hbm, live_ref),
            (target_hbm, target_ref),
            (state_hbm, state_ref),
            (source_hbm, source_ref),
            (inner_one_hbm, inner_one_ref),
            (outer_one_hbm, outer_one_ref),
            (gain_one_hbm, gain_one_ref),
            (inner_two_hbm, inner_two_ref),
            (outer_two_hbm, outer_two_ref),
            (gain_two_hbm, gain_two_ref),
        )
    ):
        load = pltpu.make_async_copy(far, near, local_sems.at[i])
        load.start()
        loads.append(load)
    for load in loads[:3]:
        load.wait()

    live = live_ref[0, 0]
    alive = lax.broadcasted_iota(jnp.int32, (1, rows), 1) < live

    def index_of(index_ref):
        return jnp.where(alive, index_ref[...], -1)

    def scatter(part, values_ref, index_ref, block):
        atom = lax.broadcasted_iota(jnp.int32, (BLOCK, rows), 0) + block * BLOCK
        ones = jnp.where(atom == index_of(index_ref), F32(1), F32(0)).astype(BF16)
        part[pl.ds(block * BLOCK, BLOCK)] = jnp.dot(ones, values_ref[...], preferred_element_type=F32)

    def mark(ones_ref, index_ref):
        for t in range(rows // LANES):
            row = jnp.where(
                lax.broadcasted_iota(jnp.int32, (1, LANES), 1) + t * LANES < live,
                index_ref[:, pl.ds(t * LANES, LANES)],
                -1,
            )
            column = jnp.transpose(jnp.broadcast_to(row, (LANES, LANES)))
            lane = lax.broadcasted_iota(jnp.int32, (LANES, LANES), 1)
            for j in range(atoms // LANES):
                ones_ref[pl.ds(t * LANES, LANES), pl.ds(j * LANES, LANES)] = jnp.where(
                    column == lane + j * LANES, F32(1), F32(0)
                ).astype(BF16)

    def pick(full, ones_ref, place, t):
        ones = ones_ref[pl.ds(t * TILE, TILE), pl.ds(place * CHUNK, CHUNK)]
        return jnp.dot(jnp.concatenate([ones, ones], axis=1), terms[...], preferred_element_type=F32)

    def split(full, place):
        values = full[pl.ds(place * CHUNK, CHUNK)]
        upper = values.astype(BF16)
        terms[pl.ds(0, CHUNK)] = upper
        terms[pl.ds(CHUNK, CHUNK)] = (values - upper.astype(F32)).astype(BF16)

    def gather(full, ones_ref, place, values_ref, first):
        split(full, place)
        for t in range(rows // TILE):
            tile = pl.ds(t * TILE, TILE)
            total = pick(full, ones_ref, place, t)
            if first:
                message[tile] = total - values_ref[tile].astype(F32)
            else:
                message[tile] = message[tile] + total

    def layer(full, ones_ref, place, inner_ref, outer_ref, gain_ref, result_ref, after_tile=None):
        split(full, place)
        for t in range(rows // TILE):
            tile = pl.ds(t * TILE, TILE)
            m = message[tile] + pick(full, ones_ref, place, t)
            mean_square = jnp.mean(m * m, axis=-1, keepdims=True)
            normed = m * lax.rsqrt(mean_square + 1e-5) * gain_ref[...]
            activated = jnp.dot(normed.astype(BF16), inner_ref[...], preferred_element_type=F32)
            activated = jnp.maximum(activated, F32(0)).astype(BF16)
            result = normed + jnp.dot(activated, outer_ref[...], preferred_element_type=F32)
            keep = lax.broadcasted_iota(jnp.int32, (TILE, channels), 0) + t * TILE < live
            result_ref[tile] = jnp.where(keep, result, F32(0)).astype(BF16)
            if after_tile is not None:
                after_tile(tile, t)

    copies = Copies(inbox, send_sems.at[0], recv_sems)

    class LayerOne:
        def __init__(self, kind, base, size):
            self.size = size
            reduce_kind, gather_kind = kind
            eighth = size // 8
            if reduce_kind == "A":
                shard_stride, part_stride = 2 * eighth, eighth
                self.reduce_ring = self.ring(base, shard_stride, part_stride, eighth)
                self.mine = rows_at(base + y * shard_stride + parity * part_stride, eighth)
                self.theirs = rows_at(base + y * shard_stride + (1 - parity) * part_stride, eighth)
                steps = [self.ring_first, self.ring_second, self.ring_then_near, self.near_then_far]
            else:
                shard_stride, part_stride = eighth, 4 * eighth
                self.reduce_ring = self.ring(base + parity * part_stride, shard_stride, eighth // 2, eighth // 2)
                self.mine = rows_at(base + y * shard_stride + parity * part_stride, eighth)
                self.upper = rows_at(base + parity * part_stride, part_stride)
                self.lower = rows_at(base + (1 - parity) * part_stride, part_stride)
                steps = [self.near_first, self.near_then_ring, self.ring_second, self.ring_then_far]
            if gather_kind == "A":
                self.gather_ring = self.ring(base, shard_stride, part_stride, eighth)
                steps += [self.far_then_near, self.near_then_gather, self.gather_second, self.gather_end]
            else:
                self.gather_ring = self.ring(
                    base + parity * part_stride, shard_stride, eighth // 2, eighth // 2
                )
                steps += [self.far_then_gather, self.gather_second, self.near_backs, self.last_backs, self.backs_end]
            self.steps = steps

            def shard(step):
                return rows_at(base + ((y + step) % RING) * shard_stride + parity * part_stride, eighth)

            self.shard = shard

        def ring(self, *where):
            return Ring(copies, y, y_after, y_before, None, *where)

        def ring_first(self):
            self.reduce_ring.reduce_first(part_one)

        def ring_second(self):
            self.reduce_ring.reduce_second(part_one)

        def hand(self, rows, count, device):
            group = copies.group()
            return group, copies.hand(part_one, rows, count, device, group), count

        def add(self, rows, handed, result):
            group, room, count = handed
            copies.arrived(group, count)
            result[rows] = part_one[rows] + inbox[room]

        def ring_then_near(self):
            self.reduce_ring.reduce_last(part_one)
            self.near = self.hand(self.theirs, self.size // 8, z_near)

        def near_then_far(self):
            self.add(self.mine, self.near, part_one)
            self.far = self.hand(self.mine, self.size // 8, z_far)

        def near_first(self):
            self.near = self.hand(self.lower, self.size // 2, z_near)

        def near_then_ring(self):
            self.add(self.upper, self.near, part_one)
            self.reduce_ring.reduce_first(part_one)

        def ring_then_far(self):
            self.reduce_ring.reduce_last(part_one)
            self.far = self.hand(self.mine, self.size // 8, z_far)

        def far_then_near(self):
            self.add(self.mine, self.far, full_one)
            self.back = copies.group()
            copies.push(full_one, self.mine, z_near, self.back)

        def near_then_gather(self):
            copies.arrived(self.back, self.size // 8)
            self.gather_ring.gather_first(full_one)

        def gather_second(self):
            self.gather_ring.gather_second(full_one)

        def gather_end(self):
            self.gather_ring.gather_rest()

        def far_then_gather(self):
            self.add(self.mine, self.far, full_one)
            self.gather_ring.gather_first(full_one, apart=True)
            self.back = copies.group()
            copies.push(full_one, self.mine, z_near, self.back)

        def near_backs(self):
            self.gather_ring.gather_near()
            for step in (1, 3):
                copies.push(full_one, self.shard(step), z_near, self.back)

        def last_backs(self):
            self.gather_ring.gather_last()
            copies.push(full_one, self.shard(2), z_near, self.back)

        def backs_end(self):
            copies.arrived(self.back, self.size // 2)

    class LayerTwo:
        def __init__(self, kind, base, size):
            side = size // 2
            self.side, self.eighth = side, side // 8
            self.ours, self.theirs = rows_at(base + core * side, side), rows_at(base + (1 - core) * side, side)
            self.own = rows_at(base + core * side + x * (2 * self.eighth), 2 * self.eighth)
            self.ring = Ring(
                copies, x, x_after, x_before, x_across, base + core * side, 2 * self.eighth, self.eighth, self.eighth
            )
            reduce_kind, gather_kind = kind
            self.steps = [self.pair_first, self.pair_then_ring]
            if reduce_kind == "A":
                self.reduce_first, self.reduce_last = self.ring.reduce_first, self.ring.reduce_last
                self.steps.append(self.ring_second)
            else:
                self.reduce_first, self.reduce_last = self.ring.reduce_at_once, self.ring.reduce_at_once_last
            self.steps += [self.ring_then_across, self.across_then_gather]
            if gather_kind == "A":
                self.gather_first, self.gather_rest = self.ring.gather_first, self.ring.gather_rest
                self.steps.append(self.gather_second)
            else:
                self.gather_first, self.gather_rest = self.ring.gather_at_once, self.ring.gather_at_once_last
            self.steps += [self.gather_then_pair, self.pair_end]

        def pair_first(self):
            self.pair = copies.group()
            self.pair_room = copies.hand(part_two, self.theirs, self.side, sibling, self.pair)

        def pair_then_ring(self):
            copies.arrived(self.pair, self.side)
            part_two[self.ours] = part_two[self.ours] + inbox[self.pair_room]
            self.reduce_first(part_two)

        def ring_second(self):
            self.ring.reduce_second(part_two)

        def ring_then_across(self):
            self.reduce_last(part_two)
            self.across = copies.group()
            self.across_room = copies.hand(part_two, self.own, 2 * self.eighth, z_across, self.across)

        def across_then_gather(self):
            copies.arrived(self.across, 2 * self.eighth)
            full_two[self.own] = part_two[self.own] + inbox[self.across_room]
            self.gather_first(full_two)

        def gather_second(self):
            self.ring.gather_second(full_two)

        def gather_then_pair(self):
            self.gather_rest()
            self.back = copies.group()
            copies.push(full_two, self.ours, sibling, self.back)

        def pair_end(self):
            copies.arrived(self.back, self.side)

    def run(chunks, order, places, scatter_block, gather_chunk, aside=None):
        done = [0] * len(chunks)
        scattered = set()
        gathered = 0
        for i, k in enumerate(order):
            if i == len(chunks) and aside is not None:
                aside()
            block = places[k] * CHUNK // BLOCK
            if block not in scattered:
                scattered.add(block)
                scatter_block(block)
            if done[k] < len(chunks[k].steps):
                chunks[k].steps[done[k]]()
            elif i < len(order) - 1:
                gather_chunk(places[k], gathered == 0)
                gathered += 1
            done[k] += 1
        assert all(d == len(c.steps) + 1 for d, c in zip(done, chunks))
        return places[order[-1]]

    def scatter_one(block):
        scatter(part_one, state_ref, target_ref, block)
        if block == PLACE_ONE[ORDER_ONE[0]] * CHUNK // BLOCK:
            pl.semaphore_wait(barrier, len(partners))

    chunks_one = [LayerOne(kind, place * CHUNK, CHUNK) for kind, place in zip(KINDS_ONE, PLACE_ONE)]
    chunks_two = [LayerTwo(kind, place * CHUNK, CHUNK) for kind, place in zip(KINDS_TWO, PLACE_TWO)]

    def mark_both():
        for load in loads[3:]:
            load.wait()
        mark(ones_one, target_ref)
        mark(ones_two, source_ref)

    last = run(
        chunks_one,
        ORDER_ONE,
        PLACE_ONE,
        scatter_one,
        lambda place, first: gather(full_one, ones_one, place, state_ref, first),
        mark_both,
    )
    layer(full_one, ones_one, last, inner_one_ref, outer_one_ref, gain_one_ref, reverse)
    copies.all_sent()
    copies.send_sem, copies.sent = send_sems.at[1], 0

    last = run(
        chunks_two,
        ORDER_TWO,
        PLACE_TWO,
        lambda block: scatter(part_two, reverse, source_ref, block),
        lambda place, first: gather(full_two, ones_two, place, reverse, first),
    )

    stores = []

    def store(tile, t):
        stores.append(pltpu.make_async_copy(final.at[tile], out_hbm.at[tile], local_sems.at[t]))
        stores[-1].start()

    layer(full_two, ones_two, last, inner_two_ref, outer_two_ref, gain_two_ref, final, store)

    copies.all_sent()
    for copy in stores:
        copy.wait()
    assert copies.groups == GROUPS


def groups_of(kind):
    return 4 + (3 if kind[1] == "A" else 4)


def groups_of_two(kind):
    return 3 + (2 if kind[0] == "A" else 1) + (2 if kind[1] == "A" else 1)


GROUPS = sum(map(groups_of, KINDS_ONE)) + sum(map(groups_of_two, KINDS_TWO))


def body(
    edge_state,
    edge_source,
    edge_target,
    live_edges,
    inner_one,
    outer_one,
    inner_two,
    outer_two,
    gain_one,
    gain_two,
):
    rows, channels = edge_state.shape[2:]
    atoms = 1024
    operands = (
        edge_state.reshape(rows, channels),
        edge_source.reshape(1, rows),
        edge_target.reshape(1, rows),
        live_edges,
        inner_one,
        outer_one,
        inner_two,
        outer_two,
        gain_one.reshape(1, channels),
        gain_two.reshape(1, channels),
    )

    def copy_of(i, operand):
        space = pltpu.SMEM if i == 3 else pltpu.VMEM
        return space(operand.shape, operand.dtype)

    result = pl.pallas_call(
        kernel,
        out_shape=jax.ShapeDtypeStruct((rows, channels), BF16),
        in_specs=[pl.BlockSpec(memory_space=pltpu.HBM)] * len(operands),
        out_specs=pl.BlockSpec(memory_space=pltpu.HBM),
        scratch_shapes=[copy_of(i, operand) for i, operand in enumerate(operands)]
        + [
            pltpu.VMEM((atoms, channels), F32),
            pltpu.VMEM((atoms, channels), F32),
            pltpu.VMEM((atoms, channels), F32),
            pltpu.VMEM((atoms, channels), F32),
            pltpu.VMEM((rows, channels), F32),
            pltpu.VMEM((rows, channels), BF16),
            pltpu.VMEM((rows, channels), BF16),
            pltpu.VMEM((2 * CHUNK, channels), BF16),
            pltpu.VMEM((rows, atoms), BF16),
            pltpu.VMEM((rows, atoms), BF16),
            pltpu.VMEM((2 * atoms, channels), F32),
            pltpu.SemaphoreType.DMA((len(operands),)),
            pltpu.SemaphoreType.DMA((2,)),
            pltpu.SemaphoreType.DMA((GROUPS,)),
        ],
        compiler_params=pltpu.CompilerParams(
            collective_id=0, has_side_effects=True, vmem_limit_bytes=56 * 2**20
        ),
    )(*operands)
    return result.reshape(1, 1, rows, channels)


def solution(mesh):
    placed = (
        P("src", "tgt", None, None),
        P("src", "tgt", None),
        P("src", "tgt", None),
        P("src", "tgt"),
        P(),
        P(),
        P(),
        P(),
        P(),
        P(),
    )
    return jax.shard_map(
        body, mesh=mesh, in_specs=placed, out_specs=P("src", "tgt", None, None), check_vma=False
    )
```

```python
import functools

import jax
import jax.numpy as jnp
from jax import lax
from jax.experimental import pallas as pl
from jax.experimental.pallas import tpu as pltpu
from jax.sharding import PartitionSpec as P

MESH = pl.DeviceIdType.MESH
RING = 4
TILE = 512
PART = 128
BLOCK = 256
LANES = 128
BF16 = jnp.bfloat16
F32 = jnp.float32

CHUNKS_ONE = (
    ("A", "A", 128, 256),
    ("b", "A", 64, 64),
    ("b", "b", 64, 512),
    ("A", "b", 64, 576),
    ("A", "A", 64, 448),
    ("b", "A", 64, 0),
    ("b", "A", 64, 768),
    ("A", "B", 128, 640),
    ("b", "A", 64, 384),
    ("A", "b", 64, 832),
    ("A", "A", 128, 896),
    ("a", "a", 64, 128),
    ("b", "b", 64, 192),
)
CHUNKS_TWO = (
    ("a", "A", 128, 256),
    ("a", "a", 128, 128),
    ("a", "a", 128, 640),
    ("a", "A", 128, 0),
    ("a", "a", 128, 896),
    ("a", "a", 128, 768),
    ("a", "a", 128, 384),
    ("a", "a", 128, 512),
)
ORDER_ONE = (1, 11, 0, 5, 4, 12, 2, 7, 11, 0, 8, 1, 5, 4, 6, 12, 7, 10, 0, 11, 2, 1, 4, 5, 3, 9, 12, 7, 0, 10, 8, 11, 4, 1, 6, 2, 5, 3, 7, 9, 10, 12, 11, 8, 0, 3, 6, 1, 9, 4, 5, 10, 2, 7, 0, 3, 8, 5, 9, 12, 4, 6, 2, 7, 1, 0, 10, 2, 8, 7, 12, 3, 5, 9, 6, 1, 7, 11, 10, 0, 3, 8, 4, 3, 9, 6, 9, 12, 2, 10, 7, 3, 8, 4, 6, 9, 10)
ORDER_TWO = (3, 1, 0, 6, 3, 7, 6, 1, 2, 5, 0, 2, 3, 4, 6, 5, 4, 1, 0, 7, 2, 3, 5, 6, 4, 1, 7, 3, 0, 2, 5, 1, 0, 4, 1, 6, 7, 2, 5, 6, 3, 2, 5, 4, 3, 0, 7, 4, 0, 7)


class Copies:
    def __init__(self, inbox, send_sem, recv_sems):
        self.inbox, self.send_sem, self.recv_sems = inbox, send_sem, recv_sems
        self.groups = self.used = self.sent = 0

    def group(self):
        self.groups += 1
        return self.groups - 1

    def room(self, count):
        room = pl.ds(self.used, count)
        self.used += count
        return room

    def start(self, src, dst, device, group):
        self.sent += src.shape[0]
        pltpu.make_async_remote_copy(
            src_ref=src,
            dst_ref=dst,
            send_sem=self.send_sem,
            recv_sem=self.recv_sems.at[group],
            device_id=device,
            device_id_type=MESH,
        ).start()

    def push(self, ref, rows, device, group):
        self.start(ref.at[rows], ref.at[rows], device, group)

    def hand(self, ref, rows, count, device, group):
        room = self.room(count)
        self.start(ref.at[rows], self.inbox.at[room], device, group)
        return room

    def wait(self, sem, count):
        rows = self.inbox.at[pl.ds(0, count)]
        pltpu.make_async_copy(rows, rows, sem).wait()

    def arrived(self, group, count):
        self.wait(self.recv_sems.at[group], count)

    def all_sent(self):
        self.wait(self.send_sem, self.sent)


def rows_at(offset, count):
    return pl.ds(pl.multiple_of(offset, 8), count)


class Ring:
    def __init__(self, copies, me, after, before, across, base, shard_stride, part_stride, count):
        self.copies, self.me, self.after, self.before, self.across = copies, me, after, before, across
        self.base, self.shard_stride, self.part_stride, self.count = base, shard_stride, part_stride, count

    def at(self, step, part):
        shard = (self.me + step + RING) % RING
        return rows_at(self.base + shard * self.shard_stride + part * self.part_stride, self.count)

    def reduce_first(self, data):
        self.relay_group, self.reduce_group = self.copies.group(), self.copies.group()

        def hand(step, part, device, group):
            return self.copies.hand(data, self.at(step, part), self.count, device, group)

        self.relays = [hand(2, 0, self.after, self.relay_group), hand(2, 1, self.before, self.relay_group)]
        self.directs = [hand(1, 1, self.after, self.reduce_group), hand(-1, 0, self.before, self.reduce_group)]

    def reduce_second(self, data):
        self.copies.arrived(self.relay_group, 2 * self.count)
        self.seconds = []
        for way, (step, device) in enumerate(((1, self.after), (-1, self.before))):
            rows = self.at(step, way)
            data[rows] = data[rows] + self.copies.inbox[self.relays[way]]
            self.seconds.append(self.copies.hand(data, rows, self.count, device, self.reduce_group))

    def reduce_last(self, data):
        self.copies.arrived(self.reduce_group, 4 * self.count)
        inbox = self.copies.inbox
        for way in range(2):
            rows = self.at(0, way)
            data[rows] = data[rows] + inbox[self.directs[1 - way]] + inbox[self.seconds[way]]

    def gather_first(self, full, apart=False):
        low, high = self.at(0, 0), self.at(0, 1)
        self.first_group, self.near_group = self.copies.group(), self.copies.group()
        self.last_group = self.copies.group() if apart else self.near_group
        push = self.copies.push
        push(full, low, self.after, self.first_group)
        push(full, high, self.before, self.first_group)
        push(full, high, self.after, self.near_group)
        push(full, low, self.before, self.near_group)

    def gather_second(self, full):
        self.copies.arrived(self.first_group, 2 * self.count)
        self.copies.push(full, self.at(-1, 0), self.after, self.last_group)
        self.copies.push(full, self.at(1, 1), self.before, self.last_group)

    def gather_near(self):
        self.copies.arrived(self.near_group, 2 * self.count)

    def gather_last(self):
        self.copies.arrived(self.last_group, 2 * self.count)

    def gather_rest(self):
        self.copies.arrived(self.near_group, 4 * self.count)


class DirectRing(Ring):
    def shard(self, step):
        return rows_at(self.base + (self.me + step + RING) % RING * self.shard_stride, 2 * self.count)

    def reduce_first(self, data):
        self.reduce_group = self.copies.group()
        self.terms = [
            self.copies.hand(data, self.shard(step), 2 * self.count, device, self.reduce_group)
            for step, device in ((1, self.after), (-1, self.before), (2, self.across))
        ]

    def reduce_last(self, data):
        self.copies.arrived(self.reduce_group, 6 * self.count)
        rows, inbox = self.shard(0), self.copies.inbox
        data[rows] = data[rows] + inbox[self.terms[0]] + inbox[self.terms[1]] + inbox[self.terms[2]]

    def gather_first(self, full, apart=False):
        self.near_group = self.copies.group()
        self.last_group = self.copies.group() if apart else self.near_group
        own = self.shard(0)
        self.copies.push(full, own, self.after, self.near_group)
        self.copies.push(full, own, self.before, self.near_group)
        self.copies.push(full, own, self.across, self.last_group)

    def gather_near(self):
        self.copies.arrived(self.near_group, 4 * self.count)

    def gather_last(self):
        self.copies.arrived(self.last_group, 2 * self.count)

    def gather_rest(self):
        self.copies.arrived(self.near_group, 6 * self.count)


def kernel(
    state_hbm,
    source_hbm,
    target_hbm,
    live_hbm,
    inner_one_hbm,
    outer_one_hbm,
    inner_two_hbm,
    outer_two_hbm,
    gain_one_hbm,
    gain_two_hbm,
    out_hbm,
    state_ref,
    source_ref,
    target_ref,
    live_ref,
    inner_one_ref,
    outer_one_ref,
    inner_two_ref,
    outer_two_ref,
    gain_one_ref,
    gain_two_ref,
    part_one,
    part_two,
    full_one,
    full_two,
    message,
    reverse,
    final,
    terms,
    ones_one,
    ones_two,
    inbox,
    local_sems,
    send_sems,
    recv_sems,
):
    rows, channels = state_ref.shape
    atoms = part_one.shape[0]

    src, tgt = lax.axis_index("src"), lax.axis_index("tgt")
    y, z_lo = src // 4, src % 4
    z_hi, x, core = tgt // 8, (tgt // 2) % 4, tgt % 2
    y_after, y_before = (((y + 1) % 4) * 4 + z_lo, tgt), (((y + 3) % 4) * 4 + z_lo, tgt)
    y_across = (((y + 2) % 4) * 4 + z_lo, tgt)
    parity = z_lo % 2
    z_near, z_far = (y * 4 + z_lo + 1 - 2 * parity, tgt), (y * 4 + (z_lo + 2) % 4, tgt)
    sibling = (src, tgt + 1 - 2 * core)
    x_after = (src, z_hi * 8 + ((x + 1) % 4) * 2 + core)
    x_before = (src, z_hi * 8 + ((x + 3) % 4) * 2 + core)
    x_across = (src, z_hi * 8 + ((x + 2) % 4) * 2 + core)
    z_across = (src, (1 - z_hi) * 8 + x * 2 + core)

    barrier = pltpu.get_barrier_semaphore()
    partners = (y_after, y_before, y_across, z_near, z_far, sibling, x_after, x_before, x_across, z_across)
    for device in partners:
        pl.semaphore_signal(barrier, inc=1, device_id=device, device_id_type=MESH)

    loads = []
    for i, (far, near) in enumerate(
        (
            (live_hbm, live_ref),
            (target_hbm, target_ref),
            (state_hbm, state_ref),
            (source_hbm, source_ref),
            (inner_one_hbm, inner_one_ref),
            (outer_one_hbm, outer_one_ref),
            (gain_one_hbm, gain_one_ref),
            (inner_two_hbm, inner_two_ref),
            (outer_two_hbm, outer_two_ref),
            (gain_two_hbm, gain_two_ref),
        )
    ):
        load = pltpu.make_async_copy(far, near, local_sems.at[i])
        load.start()
        loads.append(load)
    for load in loads[:3]:
        load.wait()

    live = live_ref[0, 0]
    alive = lax.broadcasted_iota(jnp.int32, (1, rows), 1) < live

    def index_of(index_ref):
        return jnp.where(alive, index_ref[...], -1)

    def scatter(part, values_ref, index_ref, block):
        atom = lax.broadcasted_iota(jnp.int32, (BLOCK, rows), 0) + block * BLOCK
        ones = jnp.where(atom == index_of(index_ref), F32(1), F32(0)).astype(BF16)
        part[pl.ds(block * BLOCK, BLOCK)] = jnp.dot(ones, values_ref[...], preferred_element_type=F32)

    def mark(ones_ref, index_ref):
        for t in range(rows // LANES):
            row = jnp.where(
                lax.broadcasted_iota(jnp.int32, (1, LANES), 1) + t * LANES < live,
                index_ref[:, pl.ds(t * LANES, LANES)],
                -1,
            )
            column = jnp.transpose(jnp.broadcast_to(row, (LANES, LANES)))
            lane = lax.broadcasted_iota(jnp.int32, (LANES, LANES), 1)
            for j in range(atoms // LANES):
                ones_ref[pl.ds(t * LANES, LANES), pl.ds(j * LANES, LANES)] = jnp.where(
                    column == lane + j * LANES, F32(1), F32(0)
                ).astype(BF16)

    def pick(full, ones_ref, place, t):
        ones = ones_ref[pl.ds(t * TILE, TILE), pl.ds(place * PART, PART)]
        return jnp.dot(jnp.concatenate([ones, ones], axis=1), terms[...], preferred_element_type=F32)

    def split(full, place):
        values = full[pl.ds(place * PART, PART)]
        upper = values.astype(BF16)
        terms[pl.ds(0, PART)] = upper
        terms[pl.ds(PART, PART)] = (values - upper.astype(F32)).astype(BF16)

    def gather(full, ones_ref, place, values_ref, first):
        split(full, place)
        for t in range(rows // TILE):
            tile = pl.ds(t * TILE, TILE)
            total = pick(full, ones_ref, place, t)
            if first:
                message[tile] = total - values_ref[tile].astype(F32)
            else:
                message[tile] = message[tile] + total

    def layer(full, ones_ref, place, inner_ref, outer_ref, gain_ref, result_ref, after_tile=None):
        split(full, place)
        for t in range(rows // TILE):
            tile = pl.ds(t * TILE, TILE)
            m = message[tile] + pick(full, ones_ref, place, t)
            mean_square = jnp.mean(m * m, axis=-1, keepdims=True)
            normed = m * lax.rsqrt(mean_square + 1e-5) * gain_ref[...]
            activated = jnp.dot(normed.astype(BF16), inner_ref[...], preferred_element_type=F32)
            activated = jnp.maximum(activated, F32(0)).astype(BF16)
            result = normed + jnp.dot(activated, outer_ref[...], preferred_element_type=F32)
            keep = lax.broadcasted_iota(jnp.int32, (TILE, channels), 0) + t * TILE < live
            result_ref[tile] = jnp.where(keep, result, F32(0)).astype(BF16)
            if after_tile is not None:
                after_tile(tile, t)

    copies = Copies(inbox, send_sems.at[0], recv_sems)

    def ring_of(kind):
        return Ring if kind.isupper() else DirectRing

    class LayerOne:
        def __init__(self, reduce_kind, gather_kind, size, base):
            self.size = size
            eighth = size // 8
            relayed = [self.ring_second] if reduce_kind.isupper() else []
            if reduce_kind in "Aa":
                shard_stride, part_stride = 2 * eighth, eighth
                self.reduce_ring = self.ring(reduce_kind, base, shard_stride, part_stride, eighth)
                steps = [self.ring_first, *relayed, self.ring_then_near, self.near_then_far]
            else:
                shard_stride, part_stride = eighth, 4 * eighth
                self.reduce_ring = self.ring(
                    reduce_kind, base + parity * part_stride, shard_stride, eighth // 2, eighth // 2
                )
                self.upper = rows_at(base + parity * part_stride, part_stride)
                self.lower = rows_at(base + (1 - parity) * part_stride, part_stride)
                steps = [self.near_first, self.near_then_ring, *relayed, self.ring_then_far]
            self.mine = rows_at(base + y * shard_stride + parity * part_stride, eighth)
            self.theirs = rows_at(base + y * shard_stride + (1 - parity) * part_stride, eighth)
            relayed = [self.gather_second] if gather_kind.isupper() else []
            if gather_kind in "Aa":
                self.gather_ring = self.ring(gather_kind, base, shard_stride, part_stride, eighth)
                steps += [self.far_then_near, self.near_then_gather, *relayed, self.gather_end]
            else:
                self.gather_ring = self.ring(
                    gather_kind, base + parity * part_stride, shard_stride, eighth // 2, eighth // 2
                )
                steps += [self.far_then_gather, *relayed, self.near_backs, self.last_backs, self.backs_end]
            self.steps = steps

            def shard(step):
                return rows_at(base + ((y + step) % RING) * shard_stride + parity * part_stride, eighth)

            self.shard = shard

        def ring(self, kind, *where):
            return ring_of(kind)(copies, y, y_after, y_before, y_across, *where)

        def ring_first(self):
            self.reduce_ring.reduce_first(part_one)

        def ring_second(self):
            self.reduce_ring.reduce_second(part_one)

        def hand(self, rows, count, device):
            group = copies.group()
            return group, copies.hand(part_one, rows, count, device, group), count

        def add(self, rows, handed, result):
            group, room, count = handed
            copies.arrived(group, count)
            result[rows] = part_one[rows] + inbox[room]

        def ring_then_near(self):
            self.reduce_ring.reduce_last(part_one)
            self.near = self.hand(self.theirs, self.size // 8, z_near)

        def near_then_far(self):
            self.add(self.mine, self.near, part_one)
            self.far = self.hand(self.mine, self.size // 8, z_far)

        def near_first(self):
            self.near = self.hand(self.lower, self.size // 2, z_near)

        def near_then_ring(self):
            self.add(self.upper, self.near, part_one)
            self.reduce_ring.reduce_first(part_one)

        def ring_then_far(self):
            self.reduce_ring.reduce_last(part_one)
            self.far = self.hand(self.mine, self.size // 8, z_far)

        def far_then_near(self):
            self.add(self.mine, self.far, full_one)
            self.back = copies.group()
            copies.push(full_one, self.mine, z_near, self.back)

        def near_then_gather(self):
            copies.arrived(self.back, self.size // 8)
            self.gather_ring.gather_first(full_one)

        def gather_second(self):
            self.gather_ring.gather_second(full_one)

        def gather_end(self):
            self.gather_ring.gather_rest()

        def far_then_gather(self):
            self.add(self.mine, self.far, full_one)
            self.gather_ring.gather_first(full_one, apart=True)
            self.back = copies.group()
            copies.push(full_one, self.mine, z_near, self.back)

        def near_backs(self):
            self.gather_ring.gather_near()
            for step in (1, 3):
                copies.push(full_one, self.shard(step), z_near, self.back)

        def last_backs(self):
            self.gather_ring.gather_last()
            copies.push(full_one, self.shard(2), z_near, self.back)

        def backs_end(self):
            copies.arrived(self.back, self.size // 2)

    class LayerTwo:
        def __init__(self, reduce_kind, gather_kind, size, base):
            side, eighth = size // 2, size // 16
            base_here = base + core * side
            self.side, self.shard = side, 2 * eighth
            self.ours, self.theirs = rows_at(base_here, side), rows_at(base + (1 - core) * side, side)
            self.own = rows_at(base_here + x * self.shard, self.shard)
            self.reduce_ring, self.gather_ring = [
                ring_of(kind)(copies, x, x_after, x_before, x_across, base_here, self.shard, eighth, eighth)
                for kind in (reduce_kind, gather_kind)
            ]
            self.steps = [self.pair_first, self.pair_then_ring]
            self.steps += [self.ring_second] if reduce_kind.isupper() else []
            self.steps += [self.ring_then_across, self.across_then_gather]
            self.steps += [self.gather_second] if gather_kind.isupper() else []
            self.steps += [self.gather_then_pair, self.pair_end]

        def pair_first(self):
            self.pair = copies.group()
            self.pair_room = copies.hand(part_two, self.theirs, self.side, sibling, self.pair)

        def pair_then_ring(self):
            copies.arrived(self.pair, self.side)
            part_two[self.ours] = part_two[self.ours] + inbox[self.pair_room]
            self.reduce_ring.reduce_first(part_two)

        def ring_second(self):
            self.reduce_ring.reduce_second(part_two)

        def ring_then_across(self):
            self.reduce_ring.reduce_last(part_two)
            self.across = copies.group()
            self.across_room = copies.hand(part_two, self.own, self.shard, z_across, self.across)

        def across_then_gather(self):
            copies.arrived(self.across, self.shard)
            full_two[self.own] = part_two[self.own] + inbox[self.across_room]
            self.gather_ring.gather_first(full_two)

        def gather_second(self):
            self.gather_ring.gather_second(full_two)

        def gather_then_pair(self):
            self.gather_ring.gather_rest()
            self.back = copies.group()
            copies.push(full_two, self.ours, sibling, self.back)

        def pair_end(self):
            copies.arrived(self.back, self.side)

    def run(layer_of, chunks, order, scatter_block, gather_part, aside=None):
        made = [layer_of(*chunk) for chunk in chunks]
        sizes, bases = [chunk[2] for chunk in chunks], [chunk[3] for chunk in chunks]
        assert sum(sizes) == atoms
        done = [0] * len(chunks)
        scattered, filled, gathered = set(), {}, 0
        for i, k in enumerate(order):
            if i == len(chunks) and aside is not None:
                aside()
            block, part = bases[k] // BLOCK, bases[k] // PART
            if block not in scattered:
                scattered.add(block)
                scatter_block(block, len(scattered) == 1)
            made[k].steps[done[k]]()
            done[k] += 1
            if done[k] == len(made[k].steps):
                filled[part] = filled.get(part, 0) + sizes[k]
                if filled[part] == PART:
                    gathered += 1
                    if gathered < atoms // PART:
                        gather_part(part, gathered == 1)
                    else:
                        last = part
        assert all(d == len(m.steps) for d, m in zip(done, made))
        return last

    def scatter_one(block, first):
        scatter(part_one, state_ref, target_ref, block)
        if first:
            pl.semaphore_wait(barrier, len(partners))

    def mark_both():
        for load in loads[3:]:
            load.wait()
        mark(ones_one, target_ref)
        mark(ones_two, source_ref)

    last = run(
        LayerOne,
        CHUNKS_ONE,
        ORDER_ONE,
        scatter_one,
        lambda place, first: gather(full_one, ones_one, place, state_ref, first),
        mark_both,
    )
    layer(full_one, ones_one, last, inner_one_ref, outer_one_ref, gain_one_ref, reverse)
    copies.all_sent()
    copies.send_sem, copies.sent = send_sems.at[1], 0

    last = run(
        LayerTwo,
        CHUNKS_TWO,
        ORDER_TWO,
        lambda block, first: scatter(part_two, reverse, source_ref, block),
        lambda place, first: gather(full_two, ones_two, place, reverse, first),
    )

    stores = []

    def store(tile, t):
        stores.append(pltpu.make_async_copy(final.at[tile], out_hbm.at[tile], local_sems.at[t]))
        stores[-1].start()

    layer(full_two, ones_two, last, inner_two_ref, outer_two_ref, gain_two_ref, final, store)

    copies.all_sent()
    for copy in stores:
        copy.wait()
    assert copies.groups == GROUPS


def groups_of(reduce_kind, gather_kind, *_):
    return 5 + reduce_kind.isupper() + gather_kind.isupper() + (gather_kind in "Bb")


GROUPS = sum(groups_of(*chunk) for chunk in CHUNKS_ONE + CHUNKS_TWO)


def body(
    edge_state,
    edge_source,
    edge_target,
    live_edges,
    inner_one,
    outer_one,
    inner_two,
    outer_two,
    gain_one,
    gain_two,
):
    rows, channels = edge_state.shape[2:]
    atoms = 1024
    operands = (
        edge_state.reshape(rows, channels),
        edge_source.reshape(1, rows),
        edge_target.reshape(1, rows),
        live_edges,
        inner_one,
        outer_one,
        inner_two,
        outer_two,
        gain_one.reshape(1, channels),
        gain_two.reshape(1, channels),
    )

    def copy_of(i, operand):
        space = pltpu.SMEM if i == 3 else pltpu.VMEM
        return space(operand.shape, operand.dtype)

    result = pl.pallas_call(
        kernel,
        out_shape=jax.ShapeDtypeStruct((rows, channels), BF16),
        in_specs=[pl.BlockSpec(memory_space=pltpu.HBM)] * len(operands),
        out_specs=pl.BlockSpec(memory_space=pltpu.HBM),
        scratch_shapes=[copy_of(i, operand) for i, operand in enumerate(operands)]
        + [
            pltpu.VMEM((atoms, channels), F32),
            pltpu.VMEM((atoms, channels), F32),
            pltpu.VMEM((atoms, channels), F32),
            pltpu.VMEM((atoms, channels), F32),
            pltpu.VMEM((rows, channels), F32),
            pltpu.VMEM((rows, channels), BF16),
            pltpu.VMEM((rows, channels), BF16),
            pltpu.VMEM((2 * PART, channels), BF16),
            pltpu.VMEM((rows, atoms), BF16),
            pltpu.VMEM((rows, atoms), BF16),
            pltpu.VMEM((2 * atoms, channels), F32),
            pltpu.SemaphoreType.DMA((len(operands),)),
            pltpu.SemaphoreType.DMA((2,)),
            pltpu.SemaphoreType.DMA((GROUPS,)),
        ],
        compiler_params=pltpu.CompilerParams(
            collective_id=0, has_side_effects=True, vmem_limit_bytes=56 * 2**20
        ),
    )(*operands)
    return result.reshape(1, 1, rows, channels)


def solution(mesh):
    placed = (
        P("src", "tgt", None, None),
        P("src", "tgt", None),
        P("src", "tgt", None),
        P("src", "tgt"),
        P(),
        P(),
        P(),
        P(),
        P(),
        P(),
    )
    return jax.shard_map(
        body, mesh=mesh, in_specs=placed, out_specs=P("src", "tgt", None, None), check_vma=False
    )
```

```python
import functools

import jax
import jax.numpy as jnp
from jax import lax
from jax.experimental import pallas as pl
from jax.experimental.pallas import tpu as pltpu
from jax.sharding import PartitionSpec as P

MESH = pl.DeviceIdType.MESH
RING = 4
TILE = 512
PART = 128
BLOCK = 256
LANES = 128
BF16 = jnp.bfloat16
F32 = jnp.float32

CHUNKS_ONE = (
    ("A", "A", 64, 704),
    ("b", "A", 64, 576),
    ("A", "A", 64, 256),
    ("A", "B", 128, 384),
    ("b", "A", 64, 64),
    ("B", "B", 128, 768),
    ("A", "b", 64, 320),
    ("A", "b", 64, 192),
    ("b", "A", 64, 128),
    ("A", "a", 64, 960),
    ("A", "A", 64, 640),
    ("a", "a", 64, 0),
    ("b", "A", 64, 512),
    ("a", "b", 64, 896),
)
CHUNKS_TWO = (
    ("a", "A", 128, 256),
    ("a", "a", 128, 128),
    ("a", "a", 128, 640),
    ("a", "A", 128, 0),
    ("a", "a", 128, 896),
    ("a", "a", 128, 768),
    ("a", "a", 128, 384),
    ("a", "a", 128, 512),
)
ORDER_ONE = (11, 8, 2, 3, 7, 1, 4, 10, 0, 12, 11, 8, 2, 5, 3, 4, 7, 10, 1, 0, 11, 2, 8, 9, 3, 6, 12, 4, 7, 10, 5, 0, 2, 9, 1, 11, 6, 3, 13, 8, 7, 10, 5, 4, 9, 6, 11, 0, 12, 2, 1, 8, 5, 13, 4, 3, 6, 9, 7, 10, 2, 1, 8, 0, 12, 13, 3, 3, 4, 5, 6, 10, 9, 7, 0, 12, 7, 11, 13, 3, 4, 6, 2, 5, 10, 1, 5, 6, 0, 8, 12, 9, 7, 13, 13, 5, 10, 3, 0, 2, 6, 12, 1, 13, 9, 5)
ORDER_TWO = (3, 1, 0, 6, 3, 7, 6, 1, 2, 5, 0, 2, 3, 4, 6, 5, 4, 1, 0, 7, 2, 3, 5, 6, 4, 1, 7, 3, 0, 2, 5, 1, 0, 4, 1, 6, 7, 2, 5, 6, 3, 2, 5, 4, 3, 0, 7, 4, 0, 7)


class Copies:
    def __init__(self, inbox, send_sem, recv_sems):
        self.inbox, self.send_sem, self.recv_sems = inbox, send_sem, recv_sems
        self.groups = self.used = self.sent = 0

    def group(self):
        self.groups += 1
        return self.groups - 1

    def room(self, count):
        room = pl.ds(self.used, count)
        self.used += count
        return room

    def start(self, src, dst, device, group):
        self.sent += src.shape[0]
        pltpu.make_async_remote_copy(
            src_ref=src,
            dst_ref=dst,
            send_sem=self.send_sem,
            recv_sem=self.recv_sems.at[group],
            device_id=device,
            device_id_type=MESH,
        ).start()

    def push(self, ref, rows, device, group):
        self.start(ref.at[rows], ref.at[rows], device, group)

    def hand(self, ref, rows, count, device, group):
        room = self.room(count)
        self.start(ref.at[rows], self.inbox.at[room], device, group)
        return room

    def wait(self, sem, count):
        rows = self.inbox.at[pl.ds(0, count)]
        pltpu.make_async_copy(rows, rows, sem).wait()

    def arrived(self, group, count):
        self.wait(self.recv_sems.at[group], count)

    def all_sent(self):
        self.wait(self.send_sem, self.sent)


def rows_at(offset, count):
    return pl.ds(pl.multiple_of(offset, 8), count)


class Ring:
    def __init__(self, copies, me, after, before, across, base, shard_stride, part_stride, count):
        self.copies, self.me, self.after, self.before, self.across = copies, me, after, before, across
        self.base, self.shard_stride, self.part_stride, self.count = base, shard_stride, part_stride, count

    def at(self, step, part):
        shard = (self.me + step + RING) % RING
        return rows_at(self.base + shard * self.shard_stride + part * self.part_stride, self.count)

    def reduce_first(self, data):
        self.relay_group, self.reduce_group = self.copies.group(), self.copies.group()

        def hand(step, part, device, group):
            return self.copies.hand(data, self.at(step, part), self.count, device, group)

        self.relays = [hand(2, 0, self.after, self.relay_group), hand(2, 1, self.before, self.relay_group)]
        self.directs = [hand(1, 1, self.after, self.reduce_group), hand(-1, 0, self.before, self.reduce_group)]

    def reduce_second(self, data):
        self.copies.arrived(self.relay_group, 2 * self.count)
        self.seconds = []
        for way, (step, device) in enumerate(((1, self.after), (-1, self.before))):
            rows = self.at(step, way)
            data[rows] = data[rows] + self.copies.inbox[self.relays[way]]
            self.seconds.append(self.copies.hand(data, rows, self.count, device, self.reduce_group))

    def reduce_last(self, data):
        self.copies.arrived(self.reduce_group, 4 * self.count)
        inbox = self.copies.inbox
        for way in range(2):
            rows = self.at(0, way)
            data[rows] = data[rows] + inbox[self.directs[1 - way]] + inbox[self.seconds[way]]

    def gather_first(self, full, apart=False):
        low, high = self.at(0, 0), self.at(0, 1)
        self.first_group, self.near_group = self.copies.group(), self.copies.group()
        self.last_group = self.copies.group() if apart else self.near_group
        push = self.copies.push
        push(full, low, self.after, self.first_group)
        push(full, high, self.before, self.first_group)
        push(full, high, self.after, self.near_group)
        push(full, low, self.before, self.near_group)

    def gather_second(self, full):
        self.copies.arrived(self.first_group, 2 * self.count)
        self.copies.push(full, self.at(-1, 0), self.after, self.last_group)
        self.copies.push(full, self.at(1, 1), self.before, self.last_group)

    def gather_near(self):
        self.copies.arrived(self.near_group, 2 * self.count)

    def gather_last(self):
        self.copies.arrived(self.last_group, 2 * self.count)

    def gather_rest(self):
        self.copies.arrived(self.near_group, 4 * self.count)


class DirectRing(Ring):
    def shard(self, step):
        return rows_at(self.base + (self.me + step + RING) % RING * self.shard_stride, 2 * self.count)

    def reduce_first(self, data):
        self.reduce_group = self.copies.group()
        self.terms = [
            self.copies.hand(data, self.shard(step), 2 * self.count, device, self.reduce_group)
            for step, device in ((1, self.after), (-1, self.before), (2, self.across))
        ]

    def reduce_last(self, data):
        self.copies.arrived(self.reduce_group, 6 * self.count)
        rows, inbox = self.shard(0), self.copies.inbox
        data[rows] = data[rows] + inbox[self.terms[0]] + inbox[self.terms[1]] + inbox[self.terms[2]]

    def gather_first(self, full, apart=False):
        self.near_group = self.copies.group()
        self.last_group = self.copies.group() if apart else self.near_group
        own = self.shard(0)
        self.copies.push(full, own, self.after, self.near_group)
        self.copies.push(full, own, self.before, self.near_group)
        self.copies.push(full, own, self.across, self.last_group)

    def gather_near(self):
        self.copies.arrived(self.near_group, 4 * self.count)

    def gather_last(self):
        self.copies.arrived(self.last_group, 2 * self.count)

    def gather_rest(self):
        self.copies.arrived(self.near_group, 6 * self.count)


def kernel(
    state_hbm,
    source_hbm,
    target_hbm,
    live_hbm,
    inner_one_hbm,
    outer_one_hbm,
    inner_two_hbm,
    outer_two_hbm,
    gain_one_hbm,
    gain_two_hbm,
    out_hbm,
    state_ref,
    source_ref,
    target_ref,
    live_ref,
    inner_one_ref,
    outer_one_ref,
    inner_two_ref,
    outer_two_ref,
    gain_one_ref,
    gain_two_ref,
    part_one,
    part_two,
    full_one,
    full_two,
    message,
    reverse,
    final,
    terms,
    ones_one,
    ones_two,
    inbox,
    local_sems,
    send_sems,
    recv_sems,
):
    rows, channels = state_ref.shape
    atoms = part_one.shape[0]

    src, tgt = lax.axis_index("src"), lax.axis_index("tgt")
    y, z_lo = src // 4, src % 4
    z_hi, x, core = tgt // 8, (tgt // 2) % 4, tgt % 2
    y_after, y_before = (((y + 1) % 4) * 4 + z_lo, tgt), (((y + 3) % 4) * 4 + z_lo, tgt)
    y_across = (((y + 2) % 4) * 4 + z_lo, tgt)
    parity = z_lo % 2
    z_near, z_far = (y * 4 + z_lo + 1 - 2 * parity, tgt), (y * 4 + (z_lo + 2) % 4, tgt)
    sibling = (src, tgt + 1 - 2 * core)
    x_after = (src, z_hi * 8 + ((x + 1) % 4) * 2 + core)
    x_before = (src, z_hi * 8 + ((x + 3) % 4) * 2 + core)
    x_across = (src, z_hi * 8 + ((x + 2) % 4) * 2 + core)
    z_across = (src, (1 - z_hi) * 8 + x * 2 + core)

    barrier = pltpu.get_barrier_semaphore()
    partners = (y_after, y_before, y_across, z_near, z_far, sibling, x_after, x_before, x_across, z_across)
    for device in partners:
        pl.semaphore_signal(barrier, inc=1, device_id=device, device_id_type=MESH)

    loads = []
    for i, (far, near) in enumerate(
        (
            (live_hbm, live_ref),
            (target_hbm, target_ref),
            (state_hbm, state_ref),
            (source_hbm, source_ref),
            (inner_one_hbm, inner_one_ref),
            (outer_one_hbm, outer_one_ref),
            (gain_one_hbm, gain_one_ref),
            (inner_two_hbm, inner_two_ref),
            (outer_two_hbm, outer_two_ref),
            (gain_two_hbm, gain_two_ref),
        )
    ):
        load = pltpu.make_async_copy(far, near, local_sems.at[i])
        load.start()
        loads.append(load)
    for load in loads[:3]:
        load.wait()

    live = live_ref[0, 0]
    alive = lax.broadcasted_iota(jnp.int32, (1, rows), 1) < live

    def index_of(index_ref):
        return jnp.where(alive, index_ref[...], -1)

    def scatter(part, values_ref, index_ref, block):
        atom = lax.broadcasted_iota(jnp.int32, (BLOCK, rows), 0) + block * BLOCK
        ones = jnp.where(atom == index_of(index_ref), F32(1), F32(0)).astype(BF16)
        part[pl.ds(block * BLOCK, BLOCK)] = jnp.dot(ones, values_ref[...], preferred_element_type=F32)

    def mark(ones_ref, index_ref):
        for t in range(rows // LANES):
            row = jnp.where(
                lax.broadcasted_iota(jnp.int32, (1, LANES), 1) + t * LANES < live,
                index_ref[:, pl.ds(t * LANES, LANES)],
                -1,
            )
            column = jnp.transpose(jnp.broadcast_to(row, (LANES, LANES)))
            lane = lax.broadcasted_iota(jnp.int32, (LANES, LANES), 1)
            for j in range(atoms // LANES):
                ones_ref[pl.ds(t * LANES, LANES), pl.ds(j * LANES, LANES)] = jnp.where(
                    column == lane + j * LANES, F32(1), F32(0)
                ).astype(BF16)

    def pick(full, ones_ref, place, t):
        ones = ones_ref[pl.ds(t * TILE, TILE), pl.ds(place * PART, PART)]
        return jnp.dot(jnp.concatenate([ones, ones], axis=1), terms[...], preferred_element_type=F32)

    def split(full, place):
        values = full[pl.ds(place * PART, PART)]
        upper = values.astype(BF16)
        terms[pl.ds(0, PART)] = upper
        terms[pl.ds(PART, PART)] = (values - upper.astype(F32)).astype(BF16)

    def gather(full, ones_ref, place, values_ref, first):
        split(full, place)
        for t in range(rows // TILE):
            tile = pl.ds(t * TILE, TILE)
            total = pick(full, ones_ref, place, t)
            if first:
                message[tile] = total - values_ref[tile].astype(F32)
            else:
                message[tile] = message[tile] + total

    def layer(full, ones_ref, place, inner_ref, outer_ref, gain_ref, result_ref, after_tile=None):
        split(full, place)
        for t in range(rows // TILE):
            tile = pl.ds(t * TILE, TILE)
            m = message[tile] + pick(full, ones_ref, place, t)
            mean_square = jnp.mean(m * m, axis=-1, keepdims=True)
            normed = m * lax.rsqrt(mean_square + 1e-5) * gain_ref[...]
            activated = jnp.dot(normed.astype(BF16), inner_ref[...], preferred_element_type=F32)
            activated = jnp.maximum(activated, F32(0)).astype(BF16)
            result = normed + jnp.dot(activated, outer_ref[...], preferred_element_type=F32)
            keep = lax.broadcasted_iota(jnp.int32, (TILE, channels), 0) + t * TILE < live
            result_ref[tile] = jnp.where(keep, result, F32(0)).astype(BF16)
            if after_tile is not None:
                after_tile(tile, t)

    copies = Copies(inbox, send_sems.at[0], recv_sems)

    def ring_of(kind):
        return Ring if kind.isupper() else DirectRing

    class LayerOne:
        def __init__(self, reduce_kind, gather_kind, size, base):
            self.size = size
            eighth = size // 8
            relayed = [self.ring_second] if reduce_kind.isupper() else []
            if reduce_kind in "Aa":
                shard_stride, part_stride = 2 * eighth, eighth
                self.reduce_ring = self.ring(reduce_kind, base, shard_stride, part_stride, eighth)
                steps = [self.ring_first, *relayed, self.ring_then_near, self.near_then_far]
            else:
                shard_stride, part_stride = eighth, 4 * eighth
                self.reduce_ring = self.ring(
                    reduce_kind, base + parity * part_stride, shard_stride, eighth // 2, eighth // 2
                )
                self.upper = rows_at(base + parity * part_stride, part_stride)
                self.lower = rows_at(base + (1 - parity) * part_stride, part_stride)
                steps = [self.near_first, self.near_then_ring, *relayed, self.ring_then_far]
            self.mine = rows_at(base + y * shard_stride + parity * part_stride, eighth)
            self.theirs = rows_at(base + y * shard_stride + (1 - parity) * part_stride, eighth)
            relayed = [self.gather_second] if gather_kind.isupper() else []
            if gather_kind in "Aa":
                self.gather_ring = self.ring(gather_kind, base, shard_stride, part_stride, eighth)
                steps += [self.far_then_near, self.near_then_gather, *relayed, self.gather_end]
            else:
                self.gather_ring = self.ring(
                    gather_kind, base + parity * part_stride, shard_stride, eighth // 2, eighth // 2
                )
                steps += [self.far_then_gather, *relayed, self.near_backs, self.last_backs, self.backs_end]
            self.steps = steps

            def shard(step):
                return rows_at(base + ((y + step) % RING) * shard_stride + parity * part_stride, eighth)

            self.shard = shard

        def ring(self, kind, *where):
            return ring_of(kind)(copies, y, y_after, y_before, y_across, *where)

        def ring_first(self):
            self.reduce_ring.reduce_first(part_one)

        def ring_second(self):
            self.reduce_ring.reduce_second(part_one)

        def hand(self, rows, count, device):
            group = copies.group()
            return group, copies.hand(part_one, rows, count, device, group), count

        def add(self, rows, handed, result):
            group, room, count = handed
            copies.arrived(group, count)
            result[rows] = part_one[rows] + inbox[room]

        def ring_then_near(self):
            self.reduce_ring.reduce_last(part_one)
            self.near = self.hand(self.theirs, self.size // 8, z_near)

        def near_then_far(self):
            self.add(self.mine, self.near, part_one)
            self.far = self.hand(self.mine, self.size // 8, z_far)

        def near_first(self):
            self.near = self.hand(self.lower, self.size // 2, z_near)

        def near_then_ring(self):
            self.add(self.upper, self.near, part_one)
            self.reduce_ring.reduce_first(part_one)

        def ring_then_far(self):
            self.reduce_ring.reduce_last(part_one)
            self.far = self.hand(self.mine, self.size // 8, z_far)

        def far_then_near(self):
            self.add(self.mine, self.far, full_one)
            self.back = copies.group()
            copies.push(full_one, self.mine, z_near, self.back)

        def near_then_gather(self):
            copies.arrived(self.back, self.size // 8)
            self.gather_ring.gather_first(full_one)

        def gather_second(self):
            self.gather_ring.gather_second(full_one)

        def gather_end(self):
            self.gather_ring.gather_rest()

        def far_then_gather(self):
            self.add(self.mine, self.far, full_one)
            self.gather_ring.gather_first(full_one, apart=True)
            self.back = copies.group()
            copies.push(full_one, self.mine, z_near, self.back)

        def near_backs(self):
            self.gather_ring.gather_near()
            for step in (1, 3):
                copies.push(full_one, self.shard(step), z_near, self.back)

        def last_backs(self):
            self.gather_ring.gather_last()
            copies.push(full_one, self.shard(2), z_near, self.back)

        def backs_end(self):
            copies.arrived(self.back, self.size // 2)

    class LayerTwo:
        def __init__(self, reduce_kind, gather_kind, size, base):
            side, eighth = size // 2, size // 16
            base_here = base + core * side
            self.side, self.shard = side, 2 * eighth
            self.ours, self.theirs = rows_at(base_here, side), rows_at(base + (1 - core) * side, side)
            self.own = rows_at(base_here + x * self.shard, self.shard)
            self.reduce_ring, self.gather_ring = [
                ring_of(kind)(copies, x, x_after, x_before, x_across, base_here, self.shard, eighth, eighth)
                for kind in (reduce_kind, gather_kind)
            ]
            self.steps = [self.pair_first, self.pair_then_ring]
            self.steps += [self.ring_second] if reduce_kind.isupper() else []
            self.steps += [self.ring_then_across, self.across_then_gather]
            self.steps += [self.gather_second] if gather_kind.isupper() else []
            self.steps += [self.gather_then_pair, self.pair_end]

        def pair_first(self):
            self.pair = copies.group()
            self.pair_room = copies.hand(part_two, self.theirs, self.side, sibling, self.pair)

        def pair_then_ring(self):
            copies.arrived(self.pair, self.side)
            part_two[self.ours] = part_two[self.ours] + inbox[self.pair_room]
            self.reduce_ring.reduce_first(part_two)

        def ring_second(self):
            self.reduce_ring.reduce_second(part_two)

        def ring_then_across(self):
            self.reduce_ring.reduce_last(part_two)
            self.across = copies.group()
            self.across_room = copies.hand(part_two, self.own, self.shard, z_across, self.across)

        def across_then_gather(self):
            copies.arrived(self.across, self.shard)
            full_two[self.own] = part_two[self.own] + inbox[self.across_room]
            self.gather_ring.gather_first(full_two)

        def gather_second(self):
            self.gather_ring.gather_second(full_two)

        def gather_then_pair(self):
            self.gather_ring.gather_rest()
            self.back = copies.group()
            copies.push(full_two, self.ours, sibling, self.back)

        def pair_end(self):
            copies.arrived(self.back, self.side)

    def run(layer_of, chunks, order, scatter_block, gather_part, aside=None):
        made = [layer_of(*chunk) for chunk in chunks]
        sizes, bases = [chunk[2] for chunk in chunks], [chunk[3] for chunk in chunks]
        assert sum(sizes) == atoms
        done = [0] * len(chunks)
        scattered, filled, gathered = set(), {}, 0
        for i, k in enumerate(order):
            if i == len(chunks) and aside is not None:
                aside()
            block, part = bases[k] // BLOCK, bases[k] // PART
            if block not in scattered:
                scattered.add(block)
                scatter_block(block, len(scattered) == 1)
            made[k].steps[done[k]]()
            done[k] += 1
            if done[k] == len(made[k].steps):
                filled[part] = filled.get(part, 0) + sizes[k]
                if filled[part] == PART:
                    gathered += 1
                    if gathered < atoms // PART:
                        gather_part(part, gathered == 1)
                    else:
                        last = part
        assert all(d == len(m.steps) for d, m in zip(done, made))
        return last

    def scatter_one(block, first):
        scatter(part_one, state_ref, target_ref, block)
        if first:
            pl.semaphore_wait(barrier, len(partners))

    def mark_both():
        for load in loads[3:]:
            load.wait()
        mark(ones_one, target_ref)
        mark(ones_two, source_ref)

    last = run(
        LayerOne,
        CHUNKS_ONE,
        ORDER_ONE,
        scatter_one,
        lambda place, first: gather(full_one, ones_one, place, state_ref, first),
        mark_both,
    )
    layer(full_one, ones_one, last, inner_one_ref, outer_one_ref, gain_one_ref, reverse)
    copies.all_sent()
    copies.send_sem, copies.sent = send_sems.at[1], 0

    last = run(
        LayerTwo,
        CHUNKS_TWO,
        ORDER_TWO,
        lambda block, first: scatter(part_two, reverse, source_ref, block),
        lambda place, first: gather(full_two, ones_two, place, reverse, first),
    )

    stores = []

    def store(tile, t):
        stores.append(pltpu.make_async_copy(final.at[tile], out_hbm.at[tile], local_sems.at[t]))
        stores[-1].start()

    layer(full_two, ones_two, last, inner_two_ref, outer_two_ref, gain_two_ref, final, store)

    copies.all_sent()
    for copy in stores:
        copy.wait()
    assert copies.groups == GROUPS


def groups_of(reduce_kind, gather_kind, *_):
    return 5 + reduce_kind.isupper() + gather_kind.isupper() + (gather_kind in "Bb")


GROUPS = sum(groups_of(*chunk) for chunk in CHUNKS_ONE + CHUNKS_TWO)


def body(
    edge_state,
    edge_source,
    edge_target,
    live_edges,
    inner_one,
    outer_one,
    inner_two,
    outer_two,
    gain_one,
    gain_two,
):
    rows, channels = edge_state.shape[2:]
    atoms = 1024
    operands = (
        edge_state.reshape(rows, channels),
        edge_source.reshape(1, rows),
        edge_target.reshape(1, rows),
        live_edges,
        inner_one,
        outer_one,
        inner_two,
        outer_two,
        gain_one.reshape(1, channels),
        gain_two.reshape(1, channels),
    )

    def copy_of(i, operand):
        space = pltpu.SMEM if i == 3 else pltpu.VMEM
        return space(operand.shape, operand.dtype)

    result = pl.pallas_call(
        kernel,
        out_shape=jax.ShapeDtypeStruct((rows, channels), BF16),
        in_specs=[pl.BlockSpec(memory_space=pltpu.HBM)] * len(operands),
        out_specs=pl.BlockSpec(memory_space=pltpu.HBM),
        scratch_shapes=[copy_of(i, operand) for i, operand in enumerate(operands)]
        + [
            pltpu.VMEM((atoms, channels), F32),
            pltpu.VMEM((atoms, channels), F32),
            pltpu.VMEM((atoms, channels), F32),
            pltpu.VMEM((atoms, channels), F32),
            pltpu.VMEM((rows, channels), F32),
            pltpu.VMEM((rows, channels), BF16),
            pltpu.VMEM((rows, channels), BF16),
            pltpu.VMEM((2 * PART, channels), BF16),
            pltpu.VMEM((rows, atoms), BF16),
            pltpu.VMEM((rows, atoms), BF16),
            pltpu.VMEM((2 * atoms, channels), F32),
            pltpu.SemaphoreType.DMA((len(operands),)),
            pltpu.SemaphoreType.DMA((2,)),
            pltpu.SemaphoreType.DMA((GROUPS,)),
        ],
        compiler_params=pltpu.CompilerParams(
            collective_id=0, has_side_effects=True, vmem_limit_bytes=56 * 2**20
        ),
    )(*operands)
    return result.reshape(1, 1, rows, channels)


def solution(mesh):
    placed = (
        P("src", "tgt", None, None),
        P("src", "tgt", None),
        P("src", "tgt", None),
        P("src", "tgt"),
        P(),
        P(),
        P(),
        P(),
        P(),
        P(),
    )
    return jax.shard_map(
        body, mesh=mesh, in_specs=placed, out_specs=P("src", "tgt", None, None), check_vma=False
    )
```

```python
import functools

import jax
import jax.numpy as jnp
from jax import lax
from jax.experimental import pallas as pl
from jax.experimental.pallas import tpu as pltpu
from jax.sharding import PartitionSpec as P

MESH = pl.DeviceIdType.MESH
RING = 4
TILE = 512
PART = 128
BLOCK = 256
LANES = 128
BF16 = jnp.bfloat16
F32 = jnp.float32

CHUNKS_ONE = (
    ("A", "A", 64, 704),
    ("b", "A", 64, 576),
    ("A", "A", 64, 256),
    ("A", "B", 128, 384),
    ("b", "A", 64, 64),
    ("B", "B", 128, 768),
    ("A", "b", 64, 320),
    ("A", "b", 64, 192),
    ("b", "A", 64, 128),
    ("A", "a", 64, 960),
    ("A", "A", 64, 640),
    ("a", "a", 64, 0),
    ("b", "A", 64, 512),
    ("a", "b", 64, 896),
)
CHUNKS_TWO = (
    ("a", "A", 128, 256),
    ("a", "a", 128, 128),
    ("a", "a", 128, 640),
    ("a", "A", 128, 0),
    ("a", "a", 128, 896),
    ("a", "a", 128, 768),
    ("a", "a", 128, 384),
    ("a", "a", 128, 512),
)
ORDER_ONE = (11, 8, 2, 3, 7, 1, 4, 10, 0, 12, 11, 8, 2, 5, 3, 4, 7, 10, 1, 0, 11, 2, 8, 9, 3, 6, 12, 4, 7, 10, 5, 0, 2, 9, 1, 11, 6, 3, 13, 8, 7, 10, 5, 4, 9, 6, 11, 0, 12, 2, 1, 8, 5, 13, 4, 3, 6, 9, 7, 10, 2, 1, 8, 0, 12, 13, 3, 3, 4, 5, 6, 10, 9, 7, 0, 12, 7, 11, 13, 3, 4, 6, 2, 5, 10, 1, 5, 6, 0, 8, 12, 9, 7, 13, 13, 5, 10, 3, 0, 2, 6, 12, 1, 13, 9, 5)
ORDER_TWO = (3, 1, 0, 6, 3, 7, 6, 1, 2, 5, 0, 2, 3, 4, 6, 5, 4, 1, 0, 7, 2, 3, 5, 6, 4, 1, 7, 3, 0, 2, 5, 1, 0, 4, 1, 6, 7, 2, 5, 6, 3, 2, 5, 4, 3, 0, 7, 4, 0, 7)


class Copies:
    def __init__(self, inbox, send_sem, recv_sems):
        self.inbox, self.send_sem, self.recv_sems = inbox, send_sem, recv_sems
        self.groups = self.used = self.sent = 0

    def group(self):
        self.groups += 1
        return self.groups - 1

    def room(self, count):
        room = pl.ds(self.used, count)
        self.used += count
        return room

    def start(self, src, dst, device, group):
        self.sent += src.shape[0]
        pltpu.make_async_remote_copy(
            src_ref=src,
            dst_ref=dst,
            send_sem=self.send_sem,
            recv_sem=self.recv_sems.at[group],
            device_id=device,
            device_id_type=MESH,
        ).start()

    def push(self, ref, rows, device, group):
        self.start(ref.at[rows], ref.at[rows], device, group)

    def hand(self, ref, rows, count, device, group):
        room = self.room(count)
        self.start(ref.at[rows], self.inbox.at[room], device, group)
        return room

    def wait(self, sem, count):
        rows = self.inbox.at[pl.ds(0, count)]
        pltpu.make_async_copy(rows, rows, sem).wait()

    def arrived(self, group, count):
        self.wait(self.recv_sems.at[group], count)

    def all_sent(self):
        self.wait(self.send_sem, self.sent)


def rows_at(offset, count):
    return pl.ds(pl.multiple_of(offset, 8), count)


class Ring:
    def __init__(self, copies, me, after, before, across, base, shard_stride, part_stride, count):
        self.copies, self.me, self.after, self.before, self.across = copies, me, after, before, across
        self.base, self.shard_stride, self.part_stride, self.count = base, shard_stride, part_stride, count

    def at(self, step, part):
        shard = (self.me + step + RING) % RING
        return rows_at(self.base + shard * self.shard_stride + part * self.part_stride, self.count)

    def reduce_first(self, data):
        self.relay_group, self.reduce_group = self.copies.group(), self.copies.group()

        def hand(step, part, device, group):
            return self.copies.hand(data, self.at(step, part), self.count, device, group)

        self.relays = [hand(2, 0, self.after, self.relay_group), hand(2, 1, self.before, self.relay_group)]
        self.directs = [hand(1, 1, self.after, self.reduce_group), hand(-1, 0, self.before, self.reduce_group)]

    def reduce_second(self, data):
        self.copies.arrived(self.relay_group, 2 * self.count)
        self.seconds = []
        for way, (step, device) in enumerate(((1, self.after), (-1, self.before))):
            rows = self.at(step, way)
            data[rows] = data[rows] + self.copies.inbox[self.relays[way]]
            self.seconds.append(self.copies.hand(data, rows, self.count, device, self.reduce_group))

    def reduce_last(self, data):
        self.copies.arrived(self.reduce_group, 4 * self.count)
        inbox = self.copies.inbox
        for way in range(2):
            rows = self.at(0, way)
            data[rows] = data[rows] + inbox[self.directs[1 - way]] + inbox[self.seconds[way]]

    def gather_first(self, full, apart=False):
        low, high = self.at(0, 0), self.at(0, 1)
        self.first_group, self.near_group = self.copies.group(), self.copies.group()
        self.last_group = self.copies.group() if apart else self.near_group
        push = self.copies.push
        push(full, low, self.after, self.first_group)
        push(full, high, self.before, self.first_group)
        push(full, high, self.after, self.near_group)
        push(full, low, self.before, self.near_group)

    def gather_second(self, full):
        self.copies.arrived(self.first_group, 2 * self.count)
        self.copies.push(full, self.at(-1, 0), self.after, self.last_group)
        self.copies.push(full, self.at(1, 1), self.before, self.last_group)

    def gather_near(self):
        self.copies.arrived(self.near_group, 2 * self.count)

    def gather_last(self):
        self.copies.arrived(self.last_group, 2 * self.count)

    def gather_rest(self):
        self.copies.arrived(self.near_group, 4 * self.count)


class DirectRing(Ring):
    def shard(self, step):
        return rows_at(self.base + (self.me + step + RING) % RING * self.shard_stride, 2 * self.count)

    def reduce_first(self, data):
        self.reduce_group = self.copies.group()
        self.terms = [
            self.copies.hand(data, self.shard(step), 2 * self.count, device, self.reduce_group)
            for step, device in ((1, self.after), (-1, self.before), (2, self.across))
        ]

    def reduce_last(self, data):
        self.copies.arrived(self.reduce_group, 6 * self.count)
        rows, inbox = self.shard(0), self.copies.inbox
        data[rows] = data[rows] + inbox[self.terms[0]] + inbox[self.terms[1]] + inbox[self.terms[2]]

    def gather_first(self, full, apart=False):
        self.near_group = self.copies.group()
        self.last_group = self.copies.group() if apart else self.near_group
        own = self.shard(0)
        self.copies.push(full, own, self.after, self.near_group)
        self.copies.push(full, own, self.before, self.near_group)
        self.copies.push(full, own, self.across, self.last_group)

    def gather_near(self):
        self.copies.arrived(self.near_group, 4 * self.count)

    def gather_last(self):
        self.copies.arrived(self.last_group, 2 * self.count)

    def gather_rest(self):
        self.copies.arrived(self.near_group, 6 * self.count)


def kernel(
    state_hbm,
    source_hbm,
    target_hbm,
    live_hbm,
    inner_one_hbm,
    outer_one_hbm,
    inner_two_hbm,
    outer_two_hbm,
    gain_one_hbm,
    gain_two_hbm,
    out_hbm,
    state_ref,
    source_ref,
    target_ref,
    live_ref,
    inner_one_ref,
    outer_one_ref,
    inner_two_ref,
    outer_two_ref,
    gain_one_ref,
    gain_two_ref,
    part_one,
    part_two,
    full_one,
    full_two,
    message,
    reverse,
    final,
    terms,
    ones_one,
    ones_two,
    inbox,
    local_sems,
    send_sems,
    recv_sems,
):
    rows, channels = state_ref.shape
    atoms = part_one.shape[0]

    src, tgt = lax.axis_index("src"), lax.axis_index("tgt")
    y, z_lo = src // 4, src % 4
    z_hi, x, core = tgt // 8, (tgt // 2) % 4, tgt % 2
    y_after, y_before = (((y + 1) % 4) * 4 + z_lo, tgt), (((y + 3) % 4) * 4 + z_lo, tgt)
    y_across = (((y + 2) % 4) * 4 + z_lo, tgt)
    parity = z_lo % 2
    z_near, z_far = (y * 4 + z_lo + 1 - 2 * parity, tgt), (y * 4 + (z_lo + 2) % 4, tgt)
    sibling = (src, tgt + 1 - 2 * core)
    x_after = (src, z_hi * 8 + ((x + 1) % 4) * 2 + core)
    x_before = (src, z_hi * 8 + ((x + 3) % 4) * 2 + core)
    x_across = (src, z_hi * 8 + ((x + 2) % 4) * 2 + core)
    z_across = (src, (1 - z_hi) * 8 + x * 2 + core)

    barrier = pltpu.get_barrier_semaphore()
    partners = (y_after, y_before, y_across, z_near, z_far, sibling, x_after, x_before, x_across, z_across)
    for device in partners:
        pl.semaphore_signal(barrier, inc=1, device_id=device, device_id_type=MESH)

    loads = []
    for i, (far, near) in enumerate(
        (
            (live_hbm, live_ref),
            (target_hbm, target_ref),
            (state_hbm, state_ref),
            (source_hbm, source_ref),
            (inner_one_hbm, inner_one_ref),
            (outer_one_hbm, outer_one_ref),
            (gain_one_hbm, gain_one_ref),
            (inner_two_hbm, inner_two_ref),
            (outer_two_hbm, outer_two_ref),
            (gain_two_hbm, gain_two_ref),
        )
    ):
        load = pltpu.make_async_copy(far, near, local_sems.at[i])
        load.start()
        loads.append(load)
    for load in loads[:3]:
        load.wait()

    live = live_ref[0, 0]
    alive = lax.broadcasted_iota(jnp.int32, (1, rows), 1) < live

    def index_of(index_ref):
        return jnp.where(alive, index_ref[...], -1)

    def scatter(part, values_ref, index_ref, block):
        atom = lax.broadcasted_iota(jnp.int32, (BLOCK, rows), 0) + block * BLOCK
        ones = jnp.where(atom == index_of(index_ref), F32(1), F32(0)).astype(BF16)
        part[pl.ds(block * BLOCK, BLOCK)] = jnp.dot(ones, values_ref[...], preferred_element_type=F32)

    def mark(ones_ref, index_ref):
        for t in range(rows // LANES):
            row = jnp.where(
                lax.broadcasted_iota(jnp.int32, (1, LANES), 1) + t * LANES < live,
                index_ref[:, pl.ds(t * LANES, LANES)],
                -1,
            )
            column = jnp.transpose(jnp.broadcast_to(row, (LANES, LANES)))
            lane = lax.broadcasted_iota(jnp.int32, (LANES, LANES), 1)
            for j in range(atoms // LANES):
                ones_ref[pl.ds(t * LANES, LANES), pl.ds(j * LANES, LANES)] = jnp.where(
                    column == lane + j * LANES, F32(1), F32(0)
                ).astype(BF16)

    def pick(full, ones_ref, place, t):
        ones = ones_ref[pl.ds(t * TILE, TILE), pl.ds(place * PART, PART)]
        return jnp.dot(jnp.concatenate([ones, ones], axis=1), terms[...], preferred_element_type=F32)

    def split(full, place):
        values = full[pl.ds(place * PART, PART)]
        upper = values.astype(BF16)
        terms[pl.ds(0, PART)] = upper
        terms[pl.ds(PART, PART)] = (values - upper.astype(F32)).astype(BF16)

    def gather(full, ones_ref, place, values_ref, first):
        split(full, place)
        for t in range(rows // TILE):
            tile = pl.ds(t * TILE, TILE)
            total = pick(full, ones_ref, place, t)
            if first:
                message[tile] = total - values_ref[tile].astype(F32)
            else:
                message[tile] = message[tile] + total

    def layer(full, ones_ref, place, inner_ref, outer_ref, gain_ref, result_ref, after_tile=None):
        split(full, place)
        for t in range(rows // TILE):
            tile = pl.ds(t * TILE, TILE)
            m = message[tile] + pick(full, ones_ref, place, t)
            mean_square = jnp.mean(m * m, axis=-1, keepdims=True)
            normed = m * lax.rsqrt(mean_square + 1e-5) * gain_ref[...]
            activated = jnp.dot(normed.astype(BF16), inner_ref[...], preferred_element_type=F32)
            activated = jnp.maximum(activated, F32(0)).astype(BF16)
            result = normed + jnp.dot(activated, outer_ref[...], preferred_element_type=F32)
            if after_tile is None:
                result_ref[tile] = result.astype(BF16)
            else:
                keep = lax.broadcasted_iota(jnp.int32, (TILE, channels), 0) + t * TILE < live
                result_ref[tile] = jnp.where(keep, result, F32(0)).astype(BF16)
                after_tile(tile, t)

    copies = Copies(inbox, send_sems.at[0], recv_sems)

    def ring_of(kind):
        return Ring if kind.isupper() else DirectRing

    class LayerOne:
        def __init__(self, reduce_kind, gather_kind, size, base):
            self.size = size
            eighth = size // 8
            relayed = [self.ring_second] if reduce_kind.isupper() else []
            if reduce_kind in "Aa":
                shard_stride, part_stride = 2 * eighth, eighth
                self.reduce_ring = self.ring(reduce_kind, base, shard_stride, part_stride, eighth)
                steps = [self.ring_first, *relayed, self.ring_then_near, self.near_then_far]
            else:
                shard_stride, part_stride = eighth, 4 * eighth
                self.reduce_ring = self.ring(
                    reduce_kind, base + parity * part_stride, shard_stride, eighth // 2, eighth // 2
                )
                self.upper = rows_at(base + parity * part_stride, part_stride)
                self.lower = rows_at(base + (1 - parity) * part_stride, part_stride)
                steps = [self.near_first, self.near_then_ring, *relayed, self.ring_then_far]
            self.mine = rows_at(base + y * shard_stride + parity * part_stride, eighth)
            self.theirs = rows_at(base + y * shard_stride + (1 - parity) * part_stride, eighth)
            relayed = [self.gather_second] if gather_kind.isupper() else []
            if gather_kind in "Aa":
                self.gather_ring = self.ring(gather_kind, base, shard_stride, part_stride, eighth)
                steps += [self.far_then_near, self.near_then_gather, *relayed, self.gather_end]
            else:
                self.gather_ring = self.ring(
                    gather_kind, base + parity * part_stride, shard_stride, eighth // 2, eighth // 2
                )
                steps += [self.far_then_gather, *relayed, self.near_backs, self.last_backs, self.backs_end]
            self.steps = steps

            def shard(step):
                return rows_at(base + ((y + step) % RING) * shard_stride + parity * part_stride, eighth)

            self.shard = shard

        def ring(self, kind, *where):
            return ring_of(kind)(copies, y, y_after, y_before, y_across, *where)

        def ring_first(self):
            self.reduce_ring.reduce_first(part_one)

        def ring_second(self):
            self.reduce_ring.reduce_second(part_one)

        def hand(self, rows, count, device):
            group = copies.group()
            return group, copies.hand(part_one, rows, count, device, group), count

        def add(self, rows, handed, result):
            group, room, count = handed
            copies.arrived(group, count)
            result[rows] = part_one[rows] + inbox[room]

        def ring_then_near(self):
            self.reduce_ring.reduce_last(part_one)
            self.near = self.hand(self.theirs, self.size // 8, z_near)

        def near_then_far(self):
            self.add(self.mine, self.near, part_one)
            self.far = self.hand(self.mine, self.size // 8, z_far)

        def near_first(self):
            self.near = self.hand(self.lower, self.size // 2, z_near)

        def near_then_ring(self):
            self.add(self.upper, self.near, part_one)
            self.reduce_ring.reduce_first(part_one)

        def ring_then_far(self):
            self.reduce_ring.reduce_last(part_one)
            self.far = self.hand(self.mine, self.size // 8, z_far)

        def far_then_near(self):
            self.add(self.mine, self.far, full_one)
            self.back = copies.group()
            copies.push(full_one, self.mine, z_near, self.back)

        def near_then_gather(self):
            copies.arrived(self.back, self.size // 8)
            self.gather_ring.gather_first(full_one)

        def gather_second(self):
            self.gather_ring.gather_second(full_one)

        def gather_end(self):
            self.gather_ring.gather_rest()

        def far_then_gather(self):
            self.add(self.mine, self.far, full_one)
            self.gather_ring.gather_first(full_one, apart=True)
            self.back = copies.group()
            copies.push(full_one, self.mine, z_near, self.back)

        def near_backs(self):
            self.gather_ring.gather_near()
            for step in (1, 3):
                copies.push(full_one, self.shard(step), z_near, self.back)

        def last_backs(self):
            self.gather_ring.gather_last()
            copies.push(full_one, self.shard(2), z_near, self.back)

        def backs_end(self):
            copies.arrived(self.back, self.size // 2)

    class LayerTwo:
        def __init__(self, reduce_kind, gather_kind, size, base):
            side, eighth = size // 2, size // 16
            base_here = base + core * side
            self.side, self.shard = side, 2 * eighth
            self.ours, self.theirs = rows_at(base_here, side), rows_at(base + (1 - core) * side, side)
            self.own = rows_at(base_here + x * self.shard, self.shard)
            self.reduce_ring, self.gather_ring = [
                ring_of(kind)(copies, x, x_after, x_before, x_across, base_here, self.shard, eighth, eighth)
                for kind in (reduce_kind, gather_kind)
            ]
            self.steps = [self.pair_first, self.pair_then_ring]
            self.steps += [self.ring_second] if reduce_kind.isupper() else []
            self.steps += [self.ring_then_across, self.across_then_gather]
            self.steps += [self.gather_second] if gather_kind.isupper() else []
            self.steps += [self.gather_then_pair, self.pair_end]

        def pair_first(self):
            self.pair = copies.group()
            self.pair_room = copies.hand(part_two, self.theirs, self.side, sibling, self.pair)

        def pair_then_ring(self):
            copies.arrived(self.pair, self.side)
            part_two[self.ours] = part_two[self.ours] + inbox[self.pair_room]
            self.reduce_ring.reduce_first(part_two)

        def ring_second(self):
            self.reduce_ring.reduce_second(part_two)

        def ring_then_across(self):
            self.reduce_ring.reduce_last(part_two)
            self.across = copies.group()
            self.across_room = copies.hand(part_two, self.own, self.shard, z_across, self.across)

        def across_then_gather(self):
            copies.arrived(self.across, self.shard)
            full_two[self.own] = part_two[self.own] + inbox[self.across_room]
            self.gather_ring.gather_first(full_two)

        def gather_second(self):
            self.gather_ring.gather_second(full_two)

        def gather_then_pair(self):
            self.gather_ring.gather_rest()
            self.back = copies.group()
            copies.push(full_two, self.ours, sibling, self.back)

        def pair_end(self):
            copies.arrived(self.back, self.side)

    def run(layer_of, chunks, order, scatter_block, gather_part, aside=None):
        made = [layer_of(*chunk) for chunk in chunks]
        sizes, bases = [chunk[2] for chunk in chunks], [chunk[3] for chunk in chunks]
        assert sum(sizes) == atoms
        done = [0] * len(chunks)
        scattered, filled, gathered = set(), {}, 0
        for i, k in enumerate(order):
            if i == len(chunks) and aside is not None:
                aside()
            block, part = bases[k] // BLOCK, bases[k] // PART
            if block not in scattered:
                scattered.add(block)
                scatter_block(block, len(scattered) == 1)
            made[k].steps[done[k]]()
            done[k] += 1
            if done[k] == len(made[k].steps):
                filled[part] = filled.get(part, 0) + sizes[k]
                if filled[part] == PART:
                    gathered += 1
                    if gathered < atoms // PART:
                        gather_part(part, gathered == 1)
                    else:
                        last = part
        assert all(d == len(m.steps) for d, m in zip(done, made))
        return last

    def scatter_one(block, first):
        scatter(part_one, state_ref, target_ref, block)
        if first:
            pl.semaphore_wait(barrier, len(partners))

    def mark_both():
        for load in loads[3:]:
            load.wait()
        mark(ones_one, target_ref)
        mark(ones_two, source_ref)

    last = run(
        LayerOne,
        CHUNKS_ONE,
        ORDER_ONE,
        scatter_one,
        lambda place, first: gather(full_one, ones_one, place, state_ref, first),
        mark_both,
    )
    layer(full_one, ones_one, last, inner_one_ref, outer_one_ref, gain_one_ref, reverse)
    copies.all_sent()
    copies.send_sem, copies.sent = send_sems.at[1], 0

    last = run(
        LayerTwo,
        CHUNKS_TWO,
        ORDER_TWO,
        lambda block, first: scatter(part_two, reverse, source_ref, block),
        lambda place, first: gather(full_two, ones_two, place, reverse, first),
    )

    stores = []

    def store(tile, t):
        stores.append(pltpu.make_async_copy(final.at[tile], out_hbm.at[tile], local_sems.at[t]))
        stores[-1].start()

    layer(full_two, ones_two, last, inner_two_ref, outer_two_ref, gain_two_ref, final, store)

    copies.all_sent()
    for copy in stores:
        copy.wait()
    assert copies.groups == GROUPS


def groups_of(reduce_kind, gather_kind, *_):
    return 5 + reduce_kind.isupper() + gather_kind.isupper() + (gather_kind in "Bb")


GROUPS = sum(groups_of(*chunk) for chunk in CHUNKS_ONE + CHUNKS_TWO)


def body(
    edge_state,
    edge_source,
    edge_target,
    live_edges,
    inner_one,
    outer_one,
    inner_two,
    outer_two,
    gain_one,
    gain_two,
):
    rows, channels = edge_state.shape[2:]
    atoms = 1024
    operands = (
        edge_state.reshape(rows, channels),
        edge_source.reshape(1, rows),
        edge_target.reshape(1, rows),
        live_edges,
        inner_one,
        outer_one,
        inner_two,
        outer_two,
        gain_one.reshape(1, channels),
        gain_two.reshape(1, channels),
    )

    def copy_of(i, operand):
        space = pltpu.SMEM if i == 3 else pltpu.VMEM
        return space(operand.shape, operand.dtype)

    result = pl.pallas_call(
        kernel,
        out_shape=jax.ShapeDtypeStruct((rows, channels), BF16),
        in_specs=[pl.BlockSpec(memory_space=pltpu.HBM)] * len(operands),
        out_specs=pl.BlockSpec(memory_space=pltpu.HBM),
        scratch_shapes=[copy_of(i, operand) for i, operand in enumerate(operands)]
        + [
            pltpu.VMEM((atoms, channels), F32),
            pltpu.VMEM((atoms, channels), F32),
            pltpu.VMEM((atoms, channels), F32),
            pltpu.VMEM((atoms, channels), F32),
            pltpu.VMEM((rows, channels), F32),
            pltpu.VMEM((rows, channels), BF16),
            pltpu.VMEM((rows, channels), BF16),
            pltpu.VMEM((2 * PART, channels), BF16),
            pltpu.VMEM((rows, atoms), BF16),
            pltpu.VMEM((rows, atoms), BF16),
            pltpu.VMEM((2 * atoms, channels), F32),
            pltpu.SemaphoreType.DMA((len(operands),)),
            pltpu.SemaphoreType.DMA((2,)),
            pltpu.SemaphoreType.DMA((GROUPS,)),
        ],
        compiler_params=pltpu.CompilerParams(
            collective_id=0, has_side_effects=True, vmem_limit_bytes=56 * 2**20
        ),
    )(*operands)
    return result.reshape(1, 1, rows, channels)


def solution(mesh):
    placed = (
        P("src", "tgt", None, None),
        P("src", "tgt", None),
        P("src", "tgt", None),
        P("src", "tgt"),
        P(),
        P(),
        P(),
        P(),
        P(),
        P(),
    )
    return jax.shard_map(
        body, mesh=mesh, in_specs=placed, out_specs=P("src", "tgt", None, None), check_vma=False
    )
```
